128 devices in a mesh: row: 8 (over z, core), col: 16 (over y, x).
Axes of the slice: x: 4, y: 4, z: 4, core: 2. Of those that a mesh axis runs over, the one named last changes fastest.
Arguments:
- single: bfloat16 [65536, 384], P(('row', 'col')), may hold values from -20 to 20
- left_weight: bfloat16 [384, 128], replicated, may hold values from -0.3125 to 0.3125
- right_weight: bfloat16 [384, 128], replicated, may hold values from -0.3125 to 0.3125
- bin_weight: bfloat16 [128, 64], replicated, may hold values from -3 to 3
- bin_bias: float32 [64], replicated, may hold values from -4 to 4
- block_tiles: int32 [128, 8, 2], P(('row', 'col')), may hold values from 0 to 511, as said below
- block_count: int32 [128], P(('row', 'col')), may hold values from 1 to 8, as said below
- teacher: bfloat16 [128, 8, 64, 128, 128], P(('row', 'col')), may hold values from 0 to 1, as said below
Outputs:
- grad_single: bfloat16 [65536, 384], P(('row', 'col'))
- grad_left: float32 [384, 128], replicated
- grad_right: float32 [384, 128], replicated
- grad_bin: float32 [128, 64], replicated
- loss: float32 [], replicated
The draws below stay inside these ranges and needn't reach their ends.
Inputs may be any that keep to these rules, and one draw needn't show every extreme that they name: `block_tiles`: for the device at mesh position (r, c), with tile t held by device t // 4 in row-major mesh order, each slot's row tile is held by a device of mesh row r and its column tile by a device of mesh column c. Slots 2m and 2m + 1 take their row tiles from one device and their column tiles from one device; different m take them from different devices, so at most two slots of a device name tiles of any one device on each side. Slots from block_count on are ignored. `block_count`: counts differ from device to device; some device holds 8 kept blocks. `teacher`: each pair's probabilities over the bins are positive and sum to one up to bfloat16 rounding.
All inputs are finite; a program needn't handle non-finite values.
Results may differ from the reference program's by a relative error of at most 0.011.
Values may be sent and summed in bfloat16 or wider, within the bound.
No kernel may reach another device: no remote copies, remote signals or barrier semaphores. Data moves between devices by JAX's collectives and lax.ppermute only.
A program may use at most 64 MiB of HBM per device.

```python
import math
import jax
import jax.numpy as jnp
from jax import lax

CS = 384
CF = 128
BINS = 64
TILE = 128
TILES_DEV = 4
SLOTS = 8
NDEV = 128
RESIDUES = 65536
N_ROW = 8
N_COL = 16


def draw_single(key, part):
    normal_key = jax.random.fold_in(key, 0)
    values = jnp.clip(jax.random.normal(normal_key, (RESIDUES, CS), jnp.float32), -6.0, 6.0)
    return values.astype(jnp.bfloat16)


def draw_bin_weight(key, part):
    normal_key = jax.random.fold_in(key, 0)
    spread = 3.0 / math.sqrt(CF)
    values = jnp.clip(jax.random.normal(normal_key, (CF, BINS), jnp.float32), -6.0, 6.0) * spread
    return values.astype(jnp.bfloat16)


def distinct_order(key, width):
    scores = jax.random.randint(key, (NDEV, width), 0, 1 << 20, jnp.int32) * width
    scores = scores + jnp.arange(width, dtype=jnp.int32)[None, :]
    return jnp.argsort(scores, axis=1).astype(jnp.int32)


def draw_block_tiles(key, part):
    first_key, second_key, third_key, fourth_key = jax.random.split(key, 4)
    device_ids = jnp.arange(NDEV, dtype=jnp.int32)[:, None]
    pair_ids = jnp.broadcast_to(jnp.arange(SLOTS, dtype=jnp.int32)[None, :] // 2, (NDEV, SLOTS))
    mesh_row = device_ids // N_COL
    mesh_col = device_ids % N_COL
    row_pick = jnp.take_along_axis(distinct_order(first_key, N_COL), pair_ids, axis=1)
    row_tile = (mesh_row * N_COL + row_pick) * TILES_DEV + jax.random.randint(second_key, (NDEV, SLOTS), 0, TILES_DEV, jnp.int32)
    col_pick = jnp.take_along_axis(distinct_order(third_key, N_ROW), pair_ids, axis=1)
    col_tile = (col_pick * N_COL + mesh_col) * TILES_DEV + jax.random.randint(fourth_key, (NDEV, SLOTS), 0, TILES_DEV, jnp.int32)
    return jnp.stack([row_tile, col_tile], axis=-1).astype(jnp.int32)


def draw_block_count(key, part):
    first_key, second_key, busy_key = jax.random.split(key, 3)
    first_draw = jax.random.randint(first_key, (NDEV,), 1, SLOTS + 1, jnp.int32)
    second_draw = jax.random.randint(second_key, (NDEV,), 1, SLOTS + 1, jnp.int32)
    counts = jnp.minimum(first_draw, second_draw)
    busiest = jax.random.randint(busy_key, (), 0, NDEV, jnp.int32)
    counts = jnp.where(jnp.arange(NDEV, dtype=jnp.int32) == busiest, SLOTS, counts)
    return counts.astype(jnp.int32)


def draw_teacher(key, part):
    first_key = jax.random.fold_in(key, 0)
    shape_all = (NDEV, SLOTS, BINS, TILE, TILE)
    scores = jnp.clip(jax.random.normal(first_key, shape_all, jnp.float32), -6.0, 6.0) * 2.5
    return jax.nn.softmax(scores, axis=2).astype(jnp.bfloat16)


def noise(rng, extent, scale, most, kind=jnp.bfloat16):
    return jnp.clip(scale * jax.random.normal(rng, extent, jnp.float32), -most, most).astype(kind)


def setup_inputs(seed: int = 0) -> dict:
    splits = jax.random.split(jax.random.key(seed), 9)
    return {
        "single": draw_single(jax.random.fold_in(splits[8], 71), 0),
        "left_weight": noise(splits[1], (CS, CF), CS ** -0.5, 0.3125),
        "right_weight": noise(splits[2], (CS, CF), CS ** -0.5, 0.3125),
        "bin_weight": draw_bin_weight(jax.random.fold_in(splits[8], 71), 0),
        "bin_bias": noise(splits[4], (BINS,), 1.0, 4.0, jnp.float32),
        "block_tiles": draw_block_tiles(jax.random.fold_in(splits[8], 71), 0),
        "block_count": draw_block_count(jax.random.fold_in(splits[8], 71), 0),
        "teacher": draw_teacher(jax.random.fold_in(splits[8], 71), 0),
    }


def block_terms(left_tile, right_tile, bin_weight, bin_bias, target_block):
    weight_wide = bin_weight.astype(jnp.float32)
    scaled = (left_tile.astype(jnp.float32)[None, :, :] * weight_wide.T[:, None, :]).astype(jnp.bfloat16)
    logits = jnp.einsum("kpc,qc->kpq", scaled, right_tile, preferred_element_type=jnp.float32)
    logits = logits + bin_bias.astype(jnp.float32)[:, None, None]
    highest = jnp.max(logits, axis=0, keepdims=True)
    shifted = logits - highest
    log_prob = shifted - jnp.log(jnp.sum(jnp.exp(shifted), axis=0, keepdims=True))
    target = target_block.astype(jnp.float32)
    cross_sum = -jnp.sum(target * log_prob)
    target_mass = jnp.sum(target, axis=0, keepdims=True)
    grad_logits = (target_mass * jnp.exp(log_prob) - target).astype(jnp.bfloat16)
    mixed_grad = jnp.einsum("kpq,qc->kpc", grad_logits, right_tile, preferred_element_type=jnp.float32)
    grad_left_tile = jnp.sum(mixed_grad * weight_wide.T[:, None, :], axis=0)
    grad_right_tile = jnp.einsum("kpq,kpc->qc", grad_logits, scaled, preferred_element_type=jnp.float32)
    grad_bin_tile = jnp.sum(mixed_grad * left_tile.astype(jnp.float32)[None, :, :], axis=1).T
    return grad_left_tile, grad_right_tile, grad_bin_tile, cross_sum


def reference(single, left_weight, right_weight, bin_weight, bin_bias, block_tiles, block_count, teacher):
    left_feat = jnp.dot(single, left_weight, preferred_element_type=jnp.float32).astype(jnp.bfloat16)
    right_feat = jnp.dot(single, right_weight, preferred_element_type=jnp.float32).astype(jnp.bfloat16)
    slot_count = block_tiles.shape[1]
    feature_width = left_feat.shape[1]
    rows_total = single.shape[0]
    flat_tiles = block_tiles.reshape(-1, 2)
    flat_live = (jnp.arange(slot_count, dtype=jnp.int32)[None, :] < block_count[:, None]).reshape(-1)
    flat_targets = teacher.reshape((-1,) + teacher.shape[2:])

    def visit_slot(carried, slot_item):
        left_rows_grad, right_rows_grad, grad_bin, cross_total = carried
        tile_pair, slot_live, target_block = slot_item
        row_start = (tile_pair[0] * TILE).astype(jnp.int32)
        col_start = (tile_pair[1] * TILE).astype(jnp.int32)
        left_tile = lax.dynamic_slice_in_dim(left_feat, row_start, TILE, 0)
        right_tile = lax.dynamic_slice_in_dim(right_feat, col_start, TILE, 0)

        def compute_block(ignored):
            return block_terms(left_tile, right_tile, bin_weight, bin_bias, target_block)

        def skip_block(ignored):
            return (jnp.zeros((TILE, feature_width), jnp.float32), jnp.zeros((TILE, feature_width), jnp.float32),
                    jnp.zeros(bin_weight.shape, jnp.float32), jnp.zeros((), jnp.float32))

        grad_left_part, grad_right_part, grad_bin_part, cross_part = lax.cond(slot_live, compute_block, skip_block, 0)
        previous = lax.dynamic_slice_in_dim(left_rows_grad, row_start, TILE, 0)
        left_rows_grad = lax.dynamic_update_slice_in_dim(left_rows_grad, previous + grad_left_part, row_start, 0)
        previous = lax.dynamic_slice_in_dim(right_rows_grad, col_start, TILE, 0)
        right_rows_grad = lax.dynamic_update_slice_in_dim(right_rows_grad, previous + grad_right_part, col_start, 0)
        return (left_rows_grad, right_rows_grad, grad_bin + grad_bin_part, cross_total + cross_part), None

    initial = (jnp.zeros((rows_total, feature_width), jnp.float32), jnp.zeros((rows_total, feature_width), jnp.float32),
               jnp.zeros(bin_weight.shape, jnp.float32), jnp.zeros((), jnp.float32))
    finals, ignored_out = lax.scan(visit_slot, initial, (flat_tiles, flat_live, flat_targets))
    left_rows_grad, right_rows_grad, grad_bin, cross_total = finals
    devices = N_ROW * N_COL
    left_wide = left_weight.astype(jnp.float32)
    right_wide = right_weight.astype(jnp.float32)
    grad_single = (jnp.dot(left_rows_grad, left_wide.T, precision=lax.Precision.HIGHEST)
                   + jnp.dot(right_rows_grad, right_wide.T, precision=lax.Precision.HIGHEST)).astype(jnp.bfloat16)
    single_wide = single.astype(jnp.float32)
    grad_left = jnp.dot(single_wide.T, left_rows_grad, precision=lax.Precision.HIGHEST) / devices
    grad_right = jnp.dot(single_wide.T, right_rows_grad, precision=lax.Precision.HIGHEST) / devices
    grad_bin_out = grad_bin / devices
    kept_blocks = jnp.sum(block_count).astype(jnp.float32)
    loss_value = cross_total / (kept_blocks * (TILE * TILE))
    return grad_single, grad_left, grad_right, grad_bin_out, loss_value
```

```python
import jax
import jax.numpy as jnp
from jax import lax
from jax.sharding import Mesh
from jax.sharding import PartitionSpec as P

AXES = ("z", "core", "y", "x")


def block_terms(left_tile, right_tile, bin_weight, bin_bias, target_block):
    weight_wide = bin_weight.astype(jnp.float32)
    scaled = (left_tile.astype(jnp.float32)[None, :, :] * weight_wide.T[:, None, :]).astype(
        jnp.bfloat16
    )
    logits = jnp.einsum("kpc,qc->kpq", scaled, right_tile, preferred_element_type=jnp.float32)
    logits = logits + bin_bias[:, None, None]
    highest = jnp.max(logits, axis=0, keepdims=True)
    shifted = logits - highest
    log_prob = shifted - jnp.log(jnp.sum(jnp.exp(shifted), axis=0, keepdims=True))
    target = target_block.astype(jnp.float32)
    cross_sum = -jnp.sum(target * log_prob)
    target_mass = jnp.sum(target, axis=0, keepdims=True)
    grad_logits = (target_mass * jnp.exp(log_prob) - target).astype(jnp.bfloat16)
    mixed_grad = jnp.einsum(
        "kpq,qc->kpc", grad_logits, right_tile, preferred_element_type=jnp.float32
    )
    grad_left_tile = jnp.sum(mixed_grad * weight_wide.T[:, None, :], axis=0)
    grad_right_tile = jnp.einsum(
        "kpq,kpc->qc", grad_logits, scaled, preferred_element_type=jnp.float32
    )
    grad_bin_tile = jnp.sum(mixed_grad * left_tile.astype(jnp.float32)[None, :, :], axis=1).T
    return (grad_left_tile, grad_right_tile, grad_bin_tile, cross_sum)


def shift(value, axis, step):
    size = lax.axis_size(axis)
    return lax.ppermute(value, axis, [(i, (i + step) % size) for i in range(size)])


def spread(value, axis):
    return jnp.stack([value] + [shift(value, axis, s) for s in range(1, lax.axis_size(axis))])


def collect(parts, axis):
    total = parts[0].astype(jnp.float32)
    for s in range(1, lax.axis_size(axis)):
        total = total + shift(parts[s].astype(jnp.bfloat16), axis, s).astype(jnp.float32)
    return total


def per_device(
    single, left_weight, right_weight, bin_weight, bin_bias, block_tiles, block_count, teacher
):
    tile = teacher.shape[-1]
    bins = bin_weight.shape[1]
    devices = lax.axis_size(AXES)
    tiles_dev = single.shape[0] // tile
    own_tiles = block_tiles[0]
    own_count = block_count[0]
    own_targets = teacher[0]
    left_wide = left_weight.astype(jnp.float32)
    right_wide = right_weight.astype(jnp.float32)
    left_local = jnp.dot(single, left_weight, preferred_element_type=jnp.float32).astype(
        jnp.bfloat16
    )
    right_local = jnp.dot(single, right_weight, preferred_element_type=jnp.float32).astype(
        jnp.bfloat16
    )
    width = left_local.shape[1]
    z, core, y, x = (lax.axis_index(a) for a in AXES)
    row_home = own_tiles[:, 0] // tiles_dev
    col_home = own_tiles[:, 1] // tiles_dev
    row_inner = own_tiles[:, 0] % tiles_dev
    col_inner = own_tiles[:, 1] % tiles_dev
    far_y = (row_home // 4 % 4 - y) % 4
    far_x = (row_home % 4 - x) % 4
    far_z = (col_home // 32 - z) % 4
    far_core = (col_home // 16 % 2 - core) % 2
    row_from = (((-far_y) % 4) * 4 + (-far_x) % 4) * tiles_dev + row_inner
    row_to = (far_y * 4 + far_x) * tiles_dev + row_inner
    col_from = (far_core * 4 + (-far_z) % 4) * tiles_dev + col_inner
    col_to = (far_core * 4 + far_z) * tiles_dev + col_inner
    row_bank = spread(spread(left_local, "x"), "y").reshape(-1, tile, width)
    col_bank = spread(spread(right_local, "z"), "core").reshape(-1, tile, width)
    initial = (
        jnp.zeros(row_bank.shape, jnp.float32),
        jnp.zeros(col_bank.shape, jnp.float32),
        jnp.zeros(bin_weight.shape, jnp.float32),
        jnp.zeros((), jnp.float32),
    )

    def block_step(slot_index, carried):
        row_acc, col_acc, part_bin, cross_total = carried
        row_spot = row_to[slot_index]
        col_spot = col_to[slot_index]
        grad_left_tile, grad_right_tile, grad_bin_tile, cross_sum = block_terms(
            row_bank[row_from[slot_index]],
            col_bank[col_from[slot_index]],
            bin_weight,
            bin_bias,
            own_targets[slot_index],
        )
        row_acc = lax.dynamic_update_index_in_dim(
            row_acc, row_acc[row_spot] + grad_left_tile, row_spot, 0
        )
        col_acc = lax.dynamic_update_index_in_dim(
            col_acc, col_acc[col_spot] + grad_right_tile, col_spot, 0
        )
        return (row_acc, col_acc, part_bin + grad_bin_tile, cross_total + cross_sum)

    row_acc, col_acc, part_bin, cross_total = lax.fori_loop(0, own_count, block_step, initial)
    rows_dev = single.shape[0]
    left_rows_grad = collect(
        collect(row_acc.reshape(4, 4, rows_dev, width), "y"), "x"
    )
    right_rows_grad = collect(
        collect(col_acc.reshape(2, 4, rows_dev, width), "core"), "z"
    )
    grad_single = (
        jnp.dot(left_rows_grad, left_wide.T, precision=lax.Precision.HIGHEST)
        + jnp.dot(right_rows_grad, right_wide.T, precision=lax.Precision.HIGHEST)
    ).astype(jnp.bfloat16)
    single_wide = single.astype(jnp.float32)
    part_left = jnp.dot(single_wide.T, left_rows_grad, precision=lax.Precision.HIGHEST)
    part_right = jnp.dot(single_wide.T, right_rows_grad, precision=lax.Precision.HIGHEST)
    depth = part_left.shape[0]
    rows_sum = 2 * depth + bins
    chunk = -(-(rows_sum + 1) // devices)
    scalars = jnp.stack([cross_total, own_count.astype(jnp.float32)])
    packed = jnp.concatenate(
        [
            part_left,
            part_right,
            part_bin.T,
            jnp.pad(scalars[None], ((0, chunk * devices - rows_sum - 1), (0, width - 2))),
        ]
    ).reshape(devices, chunk, width)
    mine = jnp.sum(lax.all_to_all(packed, AXES, 0, 0), axis=0)
    totals = lax.all_to_all(
        jnp.broadcast_to(mine[None], (devices, chunk, width)), AXES, 0, 0
    ).reshape(-1, width)
    grad_left = totals[:depth] / devices
    grad_right = totals[depth : 2 * depth] / devices
    grad_bin = totals[2 * depth : rows_sum].T / devices
    loss_value = totals[rows_sum, 0] / (totals[rows_sum, 1] * (tile * tile))
    return (grad_single, grad_left, grad_right, grad_bin, loss_value)


def solution(mesh):
    torus = Mesh(mesh.devices.reshape(4, 2, 4, 4), AXES)
    return jax.shard_map(
        per_device,
        mesh=torus,
        in_specs=(
            P(AXES, None),
            P(),
            P(),
            P(),
            P(),
            P(AXES, None, None),
            P(AXES),
            P(AXES, None, None, None, None),
        ),
        out_specs=(P(AXES, None), P(), P(), P(), P()),
        check_vma=False,
    )
```

```python
import jax
import jax.numpy as jnp
from jax import lax
from jax.experimental import pallas as pl
from jax.experimental.pallas import tpu as pltpu
from jax.sharding import Mesh
from jax.sharding import PartitionSpec as P

GROUP = 8


def blocks_kernel(
    place, count, bias, w_rows, w_wide, w_cols, left_bank, right_bank, teacher,
    row0, row1, row2, row3, col0, col1, bin_out, cross_out,
    left_tiles, right_tiles, target, logit, left_turn, right_turn, left_sum, right_sum,
    left_grads, right_grads, tile_sem, target_sem,
):
    rows_out = (row0, row1, row2, row3)
    cols_out = (col0, col1)
    slots, bins, tile, width = teacher.shape
    live = count[0]

    def target_copy(slot):
        return pltpu.make_async_copy(
            teacher.at[slot], target.at[lax.rem(slot, 2)], target_sem.at[lax.rem(slot, 2)]
        )

    def left_copy(slot):
        return pltpu.make_async_copy(
            left_bank.at[place[slot, 0]], left_tiles.at[slot], tile_sem.at[slot, 0]
        )

    def right_copy(slot):
        return pltpu.make_async_copy(
            right_bank.at[place[slot, 1]], right_tiles.at[slot], tile_sem.at[slot, 1]
        )

    for slot in range(slots):

        @pl.when(slot < live)
        def _():
            left_copy(slot).start()
            right_copy(slot).start()

    target_copy(0).start()
    for out in rows_out + cols_out:
        out[...] = jnp.zeros(out.shape, out.dtype)
    bin_out[...] = jnp.zeros(bin_out.shape, jnp.float32)
    cross_out[...] = jnp.zeros(cross_out.shape, jnp.float32)
    left_grads[...] = jnp.zeros(left_grads.shape, jnp.float32)
    right_grads[...] = jnp.zeros(right_grads.shape, jnp.float32)

    def block(slot, _):
        buf = lax.rem(slot, 2)

        @pl.when(slot + 1 < live)
        def _():
            target_copy(slot + 1).start()

        left_copy(slot).wait()
        right_copy(slot).wait()
        left = left_tiles[slot]
        right = right_tiles[slot]
        left_turn[...] = left.T
        right_turn[...] = right.T
        left_sum[...] = jnp.zeros(left_sum.shape, jnp.float32)
        right_sum[...] = jnp.zeros(right_sum.shape, jnp.float32)

        def scores(g, highest):
            left = left_tiles[slot].reshape(tile // 16, 16, width)
            for j in range(GROUP):
                k = g * GROUP + j
                scaled = (left * w_rows[k][None]).reshape(tile, width)
                value = jnp.dot(scaled, right_turn[...], preferred_element_type=jnp.float32)
                value = value + bias[k]
                logit[k] = value
                highest = jnp.maximum(highest, value)
            return highest

        highest = lax.fori_loop(
            0, bins // GROUP, scores, jnp.full((tile, tile), -jnp.inf, jnp.float32)
        )
        target_copy(slot).wait()

        STEP = 32
        ratios = []
        for p in range(0, tile, STEP):
            rows = pl.ds(p, STEP)
            top = highest[p : p + STEP]

            def soft(g, carried):
                total, mass, cross = carried
                for j in range(GROUP):
                    k = g * GROUP + j
                    value = logit[k, rows, :] - top
                    power = jnp.exp(value)
                    goal = target[buf, k, rows, :].astype(jnp.float32)
                    total = total + power
                    mass = mass + goal
                    cross = cross + goal * value
                    logit[k, rows, :] = power
                return total, mass, cross

            zero = jnp.zeros((STEP, tile), jnp.float32)
            total, mass, cross = lax.fori_loop(0, bins // GROUP, soft, (zero, zero, zero))
            cross = mass * jnp.log(total) - cross
            cross_out[...] += cross.reshape(STEP // 8, 8, tile).sum(0)
            ratios.append(mass / total)
        ratio = jnp.concatenate(ratios, 0)

        def grads(g, _):
            left_wide = left_tiles[slot].astype(jnp.float32)
            pieces, scales = [], []
            left_part = jnp.zeros((tile, width), jnp.float32)
            for j in range(GROUP):
                k = g * GROUP + j
                grad = logit[k] * ratio - target[buf, k].astype(jnp.float32)
                grad = grad.astype(jnp.bfloat16)
                mixed = jnp.dot(grad, right_tiles[slot], preferred_element_type=jnp.float32)
                left_part = left_part + (
                    mixed.reshape(tile // 8, 8, width) * w_wide[k][None]
                ).reshape(tile, width)
                bin_out[k] += (mixed * left_wide).reshape(tile // 8, 8, width).sum(0)
                pieces.append(grad)
                scales.append(left_turn[...] * w_cols[k])
            left_sum[...] += left_part
            right_sum[...] += jnp.dot(
                jnp.concatenate(scales, 1),
                jnp.concatenate(pieces, 0),
                preferred_element_type=jnp.float32,
            )
            return 0

        lax.fori_loop(0, bins // GROUP, grads, 0)
        left_grads[slot] = left_sum[...]
        right_grads[slot] = right_sum[...].T
        return 0

    lax.fori_loop(0, live, block, 0)

    def put(outs, spot, value):
        size = outs[0].shape[0]
        for n, out in enumerate(outs):

            @pl.when(spot // size == n)
            def _():
                out[lax.rem(spot, size)] = value.astype(jnp.bfloat16)

    for slot in range(0, slots, 2):
        for grads_ref, outs, field in ((left_grads, rows_out, 2), (right_grads, cols_out, 3)):
            first, second = place[slot, field], place[slot + 1, field]
            same = (slot + 1 < live) & (first == second)
            one, two = grads_ref[slot], grads_ref[slot + 1]

            @pl.when(slot < live)
            def _():
                put(outs, first, one + jnp.where(same, two, 0.0))

            @pl.when((slot + 1 < live) & (first != second))
            def _():
                put(outs, second, two)


def run_blocks(place, count, bin_weight, bin_bias, left_bank, right_bank, teacher):
    slots, bins, tile, _ = teacher.shape
    width = bin_weight.shape[0]
    turned = bin_weight.T
    w_rows = jnp.broadcast_to(turned[:, None, :], (bins, 16, width))
    w_wide = jnp.broadcast_to(turned[:, None, :].astype(jnp.float32), (bins, 8, width))
    w_cols = jnp.broadcast_to(turned[:, :, None], (bins, width, tile))
    smem = pl.BlockSpec(memory_space=pltpu.SMEM)
    vmem = pl.BlockSpec(memory_space=pltpu.VMEM)
    hbm = pl.BlockSpec(memory_space=pl.ANY)
    f32, bf16 = jnp.float32, jnp.bfloat16
    piece = jax.ShapeDtypeStruct((16, tile, width), bf16)
    return pl.pallas_call(
        blocks_kernel,
        out_shape=[piece] * 6
        + [
            jax.ShapeDtypeStruct((bins, 8, width), f32),
            jax.ShapeDtypeStruct((8, tile), f32),
        ],
        in_specs=[smem, smem, smem, vmem, vmem, vmem, hbm, hbm, hbm],
        out_specs=[vmem] * 8,
        scratch_shapes=[
            pltpu.VMEM((slots, tile, width), bf16),
            pltpu.VMEM((slots, tile, width), bf16),
            pltpu.VMEM((2, bins, tile, tile), bf16),
            pltpu.VMEM((bins, tile, tile), f32),
            pltpu.VMEM((width, tile), bf16),
            pltpu.VMEM((width, tile), bf16),
            pltpu.VMEM((tile, width), f32),
            pltpu.VMEM((width, tile), f32),
            pltpu.VMEM((slots, tile, width), f32),
            pltpu.VMEM((slots, tile, width), f32),
            pltpu.SemaphoreType.DMA((slots, 2)),
            pltpu.SemaphoreType.DMA((2,)),
        ],
        compiler_params=pltpu.CompilerParams(vmem_limit_bytes=48 * 1024 * 1024),
        cost_estimate=pl.CostEstimate(
            flops=6 * 8 * 64 * 128**3, bytes_accessed=20 * 2**20, transcendentals=8 * 2**20
        ),
    )(place, count, bin_bias, w_rows, w_wide, w_cols, left_bank, right_bank, teacher)


AXES = ("z", "core", "y", "x")


def shift(value, axis, step):
    size = lax.axis_size(axis)
    return lax.ppermute(value, axis, [(i, (i + step) % size) for i in range(size)])


def spread(value, axis):
    return jnp.stack([value] + [shift(value, axis, s) for s in range(1, lax.axis_size(axis))])


def collect(parts, axis):
    total = parts[0].astype(jnp.float32)
    for s in range(1, lax.axis_size(axis)):
        total = total + shift(parts[s].astype(jnp.bfloat16), axis, s).astype(jnp.float32)
    return total


def per_device(
    single, left_weight, right_weight, bin_weight, bin_bias, block_tiles, block_count, teacher
):
    tile = teacher.shape[-1]
    bins = bin_weight.shape[1]
    devices = lax.axis_size(AXES)
    tiles_dev = single.shape[0] // tile
    own_tiles = block_tiles[0]
    own_count = block_count[0]
    own_targets = teacher[0]
    left_wide = left_weight.astype(jnp.float32)
    right_wide = right_weight.astype(jnp.float32)
    left_local = jnp.dot(single, left_weight, preferred_element_type=jnp.float32).astype(
        jnp.bfloat16
    )
    right_local = jnp.dot(single, right_weight, preferred_element_type=jnp.float32).astype(
        jnp.bfloat16
    )
    width = left_local.shape[1]
    z, core, y, x = (lax.axis_index(a) for a in AXES)
    row_home = own_tiles[:, 0] // tiles_dev
    col_home = own_tiles[:, 1] // tiles_dev
    row_inner = own_tiles[:, 0] % tiles_dev
    col_inner = own_tiles[:, 1] % tiles_dev
    far_y = (row_home // 4 % 4 - y) % 4
    far_x = (row_home % 4 - x) % 4
    far_z = (col_home // 32 - z) % 4
    far_core = (col_home // 16 % 2 - core) % 2
    row_from = (((-far_y) % 4) * 4 + (-far_x) % 4) * tiles_dev + row_inner
    row_to = (far_y * 4 + far_x) * tiles_dev + row_inner
    col_from = (far_core * 4 + (-far_z) % 4) * tiles_dev + col_inner
    col_to = (far_core * 4 + far_z) * tiles_dev + col_inner
    row_bank = spread(spread(left_local, "x"), "y").reshape(-1, tile, width)
    col_bank = spread(spread(right_local, "z"), "core").reshape(-1, tile, width)
    place = jnp.stack([row_from, col_from, row_to, col_to], axis=1)
    row0, row1, row2, row3, col0, col1, bins_part, cross_part = run_blocks(
        place, block_count, bin_weight, bin_bias, row_bank, col_bank, own_targets
    )
    rows_dev = single.shape[0]
    left_near = collect((row0, row1, row2, row3), "y").reshape(4, rows_dev, width)
    right_near = collect((col0, col1), "core").reshape(4, rows_dev, width)
    left_rows_grad = collect(left_near, "x")
    right_rows_grad = collect(right_near, "z")
    grad_single = (
        jnp.dot(left_rows_grad, left_wide.T, precision=lax.Precision.HIGHEST)
        + jnp.dot(right_rows_grad, right_wide.T, precision=lax.Precision.HIGHEST)
    ).astype(jnp.bfloat16)
    single_wide = single.astype(jnp.float32)
    part_left = jnp.dot(single_wide.T, left_rows_grad, precision=lax.Precision.HIGHEST)
    part_right = jnp.dot(single_wide.T, right_rows_grad, precision=lax.Precision.HIGHEST)
    depth = part_left.shape[0]
    rows_sum = 2 * depth + bins
    chunk = -(-(rows_sum + 1) // devices)
    scalars = jnp.stack([jnp.sum(cross_part), own_count.astype(jnp.float32)])
    packed = jnp.concatenate(
        [
            part_left,
            part_right,
            jnp.sum(bins_part, axis=1),
            jnp.pad(scalars[None], ((0, chunk * devices - rows_sum - 1), (0, width - 2))),
        ]
    ).reshape(devices, chunk, width)
    mine = jnp.sum(lax.all_to_all(packed, AXES, 0, 0), axis=0)
    totals = lax.all_to_all(
        jnp.broadcast_to(mine[None], (devices, chunk, width)), AXES, 0, 0
    ).reshape(-1, width)
    grad_left = totals[:depth] / devices
    grad_right = totals[depth : 2 * depth] / devices
    grad_bin = totals[2 * depth : rows_sum].T / devices
    loss_value = totals[rows_sum, 0] / (totals[rows_sum, 1] * (tile * tile))
    return (grad_single, grad_left, grad_right, grad_bin, loss_value)


def solution(mesh):
    torus = Mesh(mesh.devices.reshape(4, 2, 4, 4), AXES)
    return jax.shard_map(
        per_device,
        mesh=torus,
        in_specs=(
            P(AXES, None),
            P(),
            P(),
            P(),
            P(),
            P(AXES, None, None),
            P(AXES),
            P(AXES, None, None, None, None),
        ),
        out_specs=(P(AXES, None), P(), P(), P(), P()),
        check_vma=False,
    )
```

```python
import functools
import jax
import jax.numpy as jnp
from jax import lax
from jax.experimental import pallas as pl
from jax.experimental.pallas import tpu as pltpu
from jax.sharding import Mesh
from jax.sharding import PartitionSpec as P

GROUP_SCORES = 32
GROUP_SOFT = 16
GROUP_GRADS = 32


def blocks_kernel(
    place, count, bias, w_rows, w_wide, w_cols, left0, left1, left2, left3, right0, right1, teacher,
    left_grads, right_grads, bin_out, cross_out,
    left_tiles, right_tiles, target, logit, left_turn, right_turn, left_sum, right_sum,
    tile_sem, target_sem,
):
    left_from = (left0, left1, left2, left3)
    right_from = (right0, right1)
    slots, bins, tile, width = teacher.shape
    live = count[0]

    def target_copy(slot):
        return pltpu.make_async_copy(
            teacher.at[slot], target.at[lax.rem(slot, 2)], target_sem.at[lax.rem(slot, 2)]
        )

    def left_copy(slot, n):
        return pltpu.make_async_copy(
            left_from[n].at[slot], left_tiles.at[slot], tile_sem.at[slot, 0]
        )

    def right_copy(slot, n):
        return pltpu.make_async_copy(
            right_from[n].at[place[slot, 2]], right_tiles.at[slot], tile_sem.at[slot, 1]
        )

    for slot in range(slots):
        for n in range(len(left_from)):

            @pl.when((slot < live) & (place[slot, 0] == n))
            def _():
                left_copy(slot, n).start()

        for n in range(len(right_from)):

            @pl.when((slot < live) & (place[slot, 1] == n))
            def _():
                right_copy(slot, n).start()

    target_copy(0).start()
    bin_out[...] = jnp.zeros(bin_out.shape, jnp.float32)
    cross_out[...] = jnp.zeros(cross_out.shape, jnp.float32)

    def block(slot, _):
        buf = lax.rem(slot, 2)

        @pl.when(slot + 1 < live)
        def _():
            target_copy(slot + 1).start()

        left_copy(slot, 0).wait()
        right_copy(slot, 0).wait()
        left = left_tiles[slot]
        right = right_tiles[slot]
        left_turn[...] = left.T
        right_turn[...] = right.T
        left_sum[...] = jnp.zeros(left_sum.shape, jnp.float32)
        right_sum[...] = jnp.zeros(right_sum.shape, jnp.float32)

        def scores(g, highest):
            left = left_tiles[slot].reshape(tile // 16, 16, width)
            for j in range(GROUP_SCORES):
                k = g * GROUP_SCORES + j
                scaled = (left * w_rows[k][None]).reshape(tile, width)
                value = jnp.dot(scaled, right_turn[...], preferred_element_type=jnp.float32)
                value = value + bias[k]
                logit[k] = value
                highest = jnp.maximum(highest, value)
            return highest

        highest = lax.fori_loop(
            0, bins // GROUP_SCORES, scores, jnp.full((tile, tile), -jnp.inf, jnp.float32)
        )
        target_copy(slot).wait()

        STEP = 32
        ratios = []
        for p in range(0, tile, STEP):
            rows = pl.ds(p, STEP)
            top = highest[p : p + STEP]

            def soft(g, carried):
                total, mass, cross = carried
                for j in range(GROUP_SOFT):
                    k = g * GROUP_SOFT + j
                    value = logit[k, rows, :] - top
                    power = jnp.exp(value)
                    goal = target[buf, k, rows, :].astype(jnp.float32)
                    total = total + power
                    mass = mass + goal
                    cross = cross + goal * value
                    logit[k, rows, :] = power
                return total, mass, cross

            zero = jnp.zeros((STEP, tile), jnp.float32)
            total, mass, cross = lax.fori_loop(0, bins // GROUP_SOFT, soft, (zero, zero, zero))
            cross = mass * jnp.log(total) - cross
            cross_out[...] += cross.reshape(STEP // 8, 8, tile).sum(0)
            ratios.append(mass / total)
        ratio = jnp.concatenate(ratios, 0)

        def grads(g, _):
            left_wide = left_tiles[slot].astype(jnp.float32)
            pieces, scales = [], []
            left_part = jnp.zeros((tile, width), jnp.float32)
            for j in range(GROUP_GRADS):
                k = g * GROUP_GRADS + j
                grad = logit[k] * ratio - target[buf, k].astype(jnp.float32)
                grad = grad.astype(jnp.bfloat16)
                mixed = jnp.dot(grad, right_tiles[slot], preferred_element_type=jnp.float32)
                left_part = left_part + (
                    mixed.reshape(tile // 8, 8, width) * w_wide[k][None]
                ).reshape(tile, width)
                bin_out[k] += (mixed * left_wide).reshape(tile // 8, 8, width).sum(0)
                pieces.append(grad)
                scales.append(left_turn[...] * w_cols[k])
            left_sum[...] += left_part
            right_sum[...] += jnp.dot(
                jnp.concatenate(scales, 1),
                jnp.concatenate(pieces, 0),
                preferred_element_type=jnp.float32,
            )
            return 0

        lax.fori_loop(0, bins // GROUP_GRADS, grads, 0)
        left_grads[slot] = left_sum[...].astype(jnp.bfloat16)
        right_grads[slot] = right_sum[...].T.astype(jnp.bfloat16)
        return 0

    lax.fori_loop(0, live, block, 0)


def run_blocks(place, count, bin_weight, bin_bias, left_from, right_from, teacher):
    slots, bins, tile, _ = teacher.shape
    width = bin_weight.shape[0]
    turned = bin_weight.T
    w_rows = jnp.broadcast_to(turned[:, None, :], (bins, 16, width))
    w_wide = jnp.broadcast_to(turned[:, None, :].astype(jnp.float32), (bins, 8, width))
    w_cols = jnp.broadcast_to(turned[:, :, None], (bins, width, tile))
    smem = pl.BlockSpec(memory_space=pltpu.SMEM)
    vmem = pl.BlockSpec(memory_space=pltpu.VMEM)
    hbm = pl.BlockSpec(memory_space=pl.ANY)
    f32, bf16 = jnp.float32, jnp.bfloat16
    piece = jax.ShapeDtypeStruct((slots, tile, width), bf16)
    return pl.pallas_call(
        blocks_kernel,
        out_shape=[piece] * 2
        + [
            jax.ShapeDtypeStruct((bins, 8, width), f32),
            jax.ShapeDtypeStruct((8, tile), f32),
        ],
        in_specs=[smem] * 3 + [vmem] * 3 + [hbm] * 7,
        out_specs=[vmem] * 4,
        scratch_shapes=[
            pltpu.VMEM((slots, tile, width), bf16),
            pltpu.VMEM((slots, tile, width), bf16),
            pltpu.VMEM((2, bins, tile, tile), bf16),
            pltpu.VMEM((bins, tile, tile), f32),
            pltpu.VMEM((width, tile), bf16),
            pltpu.VMEM((width, tile), bf16),
            pltpu.VMEM((tile, width), f32),
            pltpu.VMEM((width, tile), f32),
            pltpu.SemaphoreType.DMA((slots, 2)),
            pltpu.SemaphoreType.DMA((2,)),
        ],
        compiler_params=pltpu.CompilerParams(vmem_limit_bytes=48 * 1024 * 1024),
        cost_estimate=pl.CostEstimate(
            flops=6 * 8 * 64 * 128**3, bytes_accessed=20 * 2**20, transcendentals=8 * 2**20
        ),
    )(place, count, bin_bias, w_rows, w_wide, w_cols, *left_from, *right_from, teacher)


AXES = ("z", "core", "y", "x")
TILES_DEV = 4


def own_spot(info, s, slot):
    row = info[s, 2 * slot]
    col = info[s, 2 * slot + 1]
    return (
        (lax.rem(row // 16, 4), lax.rem(row // 4, 4), lax.rem(row, 4)),
        (lax.rem(col // 128, 4), lax.rem(col // 64, 2), lax.rem(col, 4)),
    )


def pick_kernel(info, here, near0, near1, near2, near3, out0, out1, out2, out3, bank):
    outs = (out0, out1, out2, out3)
    for n, near in enumerate((near0, near1, near2, near3)):
        bank[pl.ds(4 * n, 4)] = near[...]
    slots = out0.shape[0]
    for s in range(4):
        for slot in range(slots):
            (_, x, t), _ = own_spot(info, s, slot)
            spot = lax.rem(here[3] - x + 4, 4) * 4 + t
            outs[(4 - s) % 4][slot] = bank[spot]


def pick_tiles(info, here, near):
    slots = (info.shape[1] - 1) // 2
    _, tile, width = near[0].shape
    smem = pl.BlockSpec(memory_space=pltpu.SMEM)
    vmem = pl.BlockSpec(memory_space=pltpu.VMEM)
    return pl.pallas_call(
        pick_kernel,
        out_shape=[jax.ShapeDtypeStruct((slots, tile, width), near[0].dtype)] * 4,
        in_specs=[smem] * 2 + [vmem] * 4,
        out_specs=[vmem] * 4,
        scratch_shapes=[pltpu.VMEM((16, tile, width), near[0].dtype)],
        compiler_params=pltpu.CompilerParams(vmem_limit_bytes=16 * 1024 * 1024),
    )(info, here, *near)


def fold_kernel(side, info, here, *refs):
    sources, (own, far1, far2, far3, total) = refs[:-5], refs[-5:]
    total[...] = jnp.zeros(total.shape, jnp.float32)
    slots = sources[0].shape[0]
    for s, source in enumerate(sources):
        live = info[s, 2 * slots]
        for slot in range(slots):
            (y, x, t), (z, core, u) = own_spot(info, s, slot)
            if side == 0:
                mine, spot = y == here[2], lax.rem(x - here[3] + 4, 4) * 4 + t
            else:
                mine, spot = core == here[1], lax.rem(z - here[0] + 4, 4) * 4 + u

            @pl.when((slot < live) & mine)
            def _():
                total[spot] += source[slot].astype(jnp.float32)

    own[...] = total[pl.ds(0, 4)]
    for n, far in enumerate((far1, far2, far3)):
        far[...] = total[pl.ds(4 * n + 4, 4)].astype(jnp.bfloat16)


def fold_slots(side, info, here, sources):
    _, tile, width = sources[0].shape
    smem = pl.BlockSpec(memory_space=pltpu.SMEM)
    vmem = pl.BlockSpec(memory_space=pltpu.VMEM)
    far = jax.ShapeDtypeStruct((4, tile, width), jnp.bfloat16)
    return pl.pallas_call(
        functools.partial(fold_kernel, side),
        out_shape=[jax.ShapeDtypeStruct((4, tile, width), jnp.float32)] + [far] * 3,
        in_specs=[smem] * 2 + [vmem] * len(sources),
        out_specs=[vmem] * 4,
        scratch_shapes=[pltpu.VMEM((16, tile, width), jnp.float32)],
        compiler_params=pltpu.CompilerParams(vmem_limit_bytes=16 * 1024 * 1024),
    )(info, here, *sources)


def shift(value, axis, step):
    size = lax.axis_size(axis)
    return lax.ppermute(value, axis, [(i, (i + step) % size) for i in range(size)])


def ring(value, axis):
    return [shift(value, axis, s) for s in range(1, lax.axis_size(axis))]


SCALARS = 16


def split_rows(value):
    body, tail = value[:-SCALARS], value[-SCALARS:]
    high = tail.astype(jnp.bfloat16)
    low = (tail - high.astype(jnp.float32)).astype(jnp.bfloat16)
    return jnp.concatenate([body.astype(jnp.bfloat16), high, low])


def join_rows(sent):
    sent = sent.astype(jnp.float32)
    body, high, low = sent[: -2 * SCALARS], sent[-2 * SCALARS : -SCALARS], sent[-SCALARS:]
    return jnp.concatenate([body, high + low])


def add_kernel(value, sent1, sent2, sent3, out, send):
    total = value[...]
    for sent in (sent1, sent2, sent3):
        total = total + join_rows(sent[...])
    out[...] = total
    send[...] = split_rows(total)


def add_sent(value, sent):
    vmem = pl.BlockSpec(memory_space=pltpu.VMEM)
    return pl.pallas_call(
        add_kernel,
        out_shape=[
            jax.ShapeDtypeStruct(value.shape, jnp.float32),
            jax.ShapeDtypeStruct(sent[0].shape, jnp.bfloat16),
        ],
        in_specs=[vmem] * 4,
        out_specs=[vmem] * 2,
    )(value, *sent)


def per_device(
    single, left_weight, right_weight, bin_weight, bin_bias, block_tiles, block_count, teacher
):
    slots, bins, tile = teacher.shape[1:4]
    devices = lax.axis_size(AXES)
    own_tiles = block_tiles[0]
    left_wide = left_weight.astype(jnp.float32)
    right_wide = right_weight.astype(jnp.float32)
    info = jnp.concatenate([own_tiles.reshape(1, -1), block_count[None]], axis=1)
    info_y = jnp.concatenate([info] + ring(info, "y"))
    info_core = jnp.concatenate([info] + ring(info, "core"))
    left_local = jnp.dot(single, left_weight, preferred_element_type=jnp.float32).astype(
        jnp.bfloat16
    )
    right_local = jnp.dot(single, right_weight, preferred_element_type=jnp.float32).astype(
        jnp.bfloat16
    )
    rows_dev, width = left_local.shape
    left_local = left_local.reshape(-1, tile, width)
    right_local = right_local.reshape(-1, tile, width)
    here = jnp.stack([lax.axis_index(a) for a in AXES]).astype(jnp.int32)
    z, core, y = here[0], here[1], here[2]
    picked = pick_tiles(info_y, here, [left_local] + ring(left_local, "x"))
    left_from = [picked[0]] + [shift(picked[s], "y", s) for s in (1, 2, 3)]
    right_near = jnp.concatenate([right_local] + ring(right_local, "z"))
    right_from = [right_near, shift(right_near, "core", 1)]
    row, col = own_tiles[:, 0], own_tiles[:, 1]
    place = jnp.stack(
        [
            (y - row // 16 % 4) % 4,
            (core - col // 64 % 2) % 2,
            (z - col // 128 % 4) % 4 * TILES_DEV + col % TILES_DEV,
        ],
        axis=1,
    )
    left_slots, right_slots, bins_part, cross_part = run_blocks(
        place, block_count, bin_weight, bin_bias, left_from, right_from, teacher[0]
    )
    left_own, *left_far = fold_slots(0, info_y, here, [left_slots] + ring(left_slots, "y"))
    right_own, *right_far = fold_slots(
        1, info_core, here, [right_slots] + ring(right_slots, "core")
    )
    left_rows_grad, right_rows_grad = left_own, right_own
    for s in (1, 2, 3):
        left_rows_grad = left_rows_grad + shift(left_far[s - 1], "x", s).astype(jnp.float32)
        right_rows_grad = right_rows_grad + shift(right_far[s - 1], "z", s).astype(jnp.float32)
    left_rows_grad = left_rows_grad.reshape(rows_dev, width)
    right_rows_grad = right_rows_grad.reshape(rows_dev, width)
    single_wide = single.astype(jnp.float32)
    part_left = jnp.dot(single_wide.T, left_rows_grad, precision=lax.Precision.HIGHEST)
    part_right = jnp.dot(single_wide.T, right_rows_grad, precision=lax.Precision.HIGHEST)
    depth = part_left.shape[0]
    scalars = jnp.stack([jnp.sum(cross_part), block_count[0].astype(jnp.float32)])
    scalars = jnp.pad(scalars[None], ((0, SCALARS - 1), (0, width - 2)))
    part_bin = jnp.sum(bins_part, axis=1)
    first = jnp.concatenate([part_left, part_bin, jnp.zeros_like(scalars)])
    second = jnp.concatenate([part_right, jnp.zeros_like(part_bin), scalars])
    low_core = core == 0
    total = jnp.where(low_core, first, second) + shift(
        jnp.where(low_core, second, first), "core", 1
    )
    send = split_rows(total)
    for axis in ("z", "y", "x"):
        total, send = add_sent(total, ring(send, axis))
    other = shift(total, "core", 1)
    first = jnp.where(low_core, total, other)
    second = jnp.where(low_core, other, total)
    grad_single = (
        jnp.dot(left_rows_grad, left_wide.T, precision=lax.Precision.HIGHEST)
        + jnp.dot(right_rows_grad, right_wide.T, precision=lax.Precision.HIGHEST)
    ).astype(jnp.bfloat16)
    grad_left = first[:depth] / devices
    grad_right = second[:depth] / devices
    grad_bin = first[depth : depth + bins].T / devices
    loss_value = second[depth + bins, 0] / (second[depth + bins, 1] * (tile * tile))
    return (grad_single, grad_left, grad_right, grad_bin, loss_value)


def solution(mesh):
    torus = Mesh(mesh.devices.reshape(4, 2, 4, 4), AXES)
    return jax.shard_map(
        per_device,
        mesh=torus,
        in_specs=(
            P(AXES, None),
            P(),
            P(),
            P(),
            P(),
            P(AXES, None, None),
            P(AXES),
            P(AXES, None, None, None, None),
        ),
        out_specs=(P(AXES, None), P(), P(), P(), P()),
        check_vma=False,
    )
```

```python
import functools
import jax
import jax.numpy as jnp
from jax import lax
from jax.experimental import pallas as pl
from jax.experimental.pallas import tpu as pltpu
from jax.sharding import Mesh
from jax.sharding import PartitionSpec as P

GROUP_SCORES = 32
GROUP_SOFT = 16
GROUP_GRADS = 32


def blocks_kernel(
    place, count, bias, w_turned, w_plain, left0, left1, left2, left3, right0, right1, teacher,
    left_grads, right_grads, bin_out, cross_out,
    w_rows, w_wide, w_cols, left_tiles, right_tiles, target, logit, left_turn, right_turn, left_sum, right_sum,
    tile_sem, target_sem,
):
    left_from = (left0, left1, left2, left3)
    right_from = (right0, right1)
    slots, bins, tile, width = teacher.shape
    live = count[0]

    def target_copy(slot):
        return pltpu.make_async_copy(
            teacher.at[slot], target.at[lax.rem(slot, 2)], target_sem.at[lax.rem(slot, 2)]
        )

    def left_copy(slot, n):
        return pltpu.make_async_copy(
            left_from[n].at[slot], left_tiles.at[slot], tile_sem.at[slot, 0]
        )

    def right_copy(slot, n):
        return pltpu.make_async_copy(
            right_from[n].at[place[slot, 2]], right_tiles.at[slot], tile_sem.at[slot, 1]
        )

    for slot in range(slots):
        for n in range(len(left_from)):

            @pl.when((slot < live) & (place[slot, 0] == n))
            def _():
                left_copy(slot, n).start()

        for n in range(len(right_from)):

            @pl.when((slot < live) & (place[slot, 1] == n))
            def _():
                right_copy(slot, n).start()

    target_copy(0).start()
    for k in range(bins):
        row = w_turned[k : k + 1, :]
        w_wide[k] = jnp.broadcast_to(row, (8, width))
        w_rows[k] = jnp.broadcast_to(row, (16, width)).astype(jnp.bfloat16)
        w_cols[k] = jnp.broadcast_to(w_plain[:, k : k + 1], (width, tile)).astype(jnp.bfloat16)
    bin_out[...] = jnp.zeros(bin_out.shape, jnp.float32)
    cross_out[...] = jnp.zeros(cross_out.shape, jnp.float32)

    def block(slot, _):
        buf = lax.rem(slot, 2)

        @pl.when(slot + 1 < live)
        def _():
            target_copy(slot + 1).start()

        left_copy(slot, 0).wait()
        right_copy(slot, 0).wait()
        left = left_tiles[slot]
        right = right_tiles[slot]
        left_turn[...] = left.T
        right_turn[...] = right.T
        left_sum[...] = jnp.zeros(left_sum.shape, jnp.float32)
        right_sum[...] = jnp.zeros(right_sum.shape, jnp.float32)

        def scores(g, highest):
            left = left_tiles[slot].reshape(tile // 16, 16, width)
            for j in range(GROUP_SCORES):
                k = g * GROUP_SCORES + j
                scaled = (left * w_rows[k][None]).reshape(tile, width)
                value = jnp.dot(scaled, right_turn[...], preferred_element_type=jnp.float32)
                value = value + bias[k]
                logit[k] = value
                highest = jnp.maximum(highest, value)
            return highest

        highest = lax.fori_loop(
            0, bins // GROUP_SCORES, scores, jnp.full((tile, tile), -jnp.inf, jnp.float32)
        )
        target_copy(slot).wait()

        STEP = 32
        ratios = []
        for p in range(0, tile, STEP):
            rows = pl.ds(p, STEP)
            top = highest[p : p + STEP]

            def soft(g, carried):
                total, mass, cross = carried
                for j in range(GROUP_SOFT):
                    k = g * GROUP_SOFT + j
                    value = logit[k, rows, :] - top
                    power = jnp.exp(value)
                    goal = target[buf, k, rows, :].astype(jnp.float32)
                    total = total + power
                    mass = mass + goal
                    cross = cross + goal * value
                    logit[k, rows, :] = power
                return total, mass, cross

            zero = jnp.zeros((STEP, tile), jnp.float32)
            total, mass, cross = lax.fori_loop(0, bins // GROUP_SOFT, soft, (zero, zero, zero))
            cross = mass * jnp.log(total) - cross
            cross_out[...] += cross.reshape(STEP // 8, 8, tile).sum(0)
            ratios.append(mass / total)
        ratio = jnp.concatenate(ratios, 0)

        def grads(g, _):
            left_wide = left_tiles[slot].astype(jnp.float32)
            pieces, scales = [], []
            left_part = jnp.zeros((tile, width), jnp.float32)
            for j in range(GROUP_GRADS):
                k = g * GROUP_GRADS + j
                grad = logit[k] * ratio - target[buf, k].astype(jnp.float32)
                grad = grad.astype(jnp.bfloat16)
                mixed = jnp.dot(grad, right_tiles[slot], preferred_element_type=jnp.float32)
                left_part = left_part + (
                    mixed.reshape(tile // 8, 8, width) * w_wide[k][None]
                ).reshape(tile, width)
                bin_out[k] += (mixed * left_wide).reshape(tile // 8, 8, width).sum(0)
                pieces.append(grad)
                scales.append(left_turn[...] * w_cols[k])
            left_sum[...] += left_part
            right_sum[...] += jnp.dot(
                jnp.concatenate(scales, 1),
                jnp.concatenate(pieces, 0),
                preferred_element_type=jnp.float32,
            )
            return 0

        lax.fori_loop(0, bins // GROUP_GRADS, grads, 0)
        left_grads[slot] = left_sum[...].astype(jnp.bfloat16)
        right_grads[slot] = right_sum[...].T.astype(jnp.bfloat16)
        return 0

    lax.fori_loop(0, live, block, 0)


def run_blocks(place, count, bin_weight, bin_bias, left_from, right_from, teacher):
    slots, bins, tile, _ = teacher.shape
    width = bin_weight.shape[0]
    wide = bin_weight.astype(jnp.float32)
    smem = pl.BlockSpec(memory_space=pltpu.SMEM)
    vmem = pl.BlockSpec(memory_space=pltpu.VMEM)
    hbm = pl.BlockSpec(memory_space=pl.ANY)
    f32, bf16 = jnp.float32, jnp.bfloat16
    piece = jax.ShapeDtypeStruct((slots, tile, width), bf16)
    return pl.pallas_call(
        blocks_kernel,
        out_shape=[piece] * 2
        + [
            jax.ShapeDtypeStruct((bins, 8, width), f32),
            jax.ShapeDtypeStruct((8, tile), f32),
        ],
        in_specs=[smem] * 3 + [vmem] * 2 + [hbm] * 7,
        out_specs=[vmem] * 4,
        scratch_shapes=[
            pltpu.VMEM((bins, 16, width), bf16),
            pltpu.VMEM((bins, 8, width), f32),
            pltpu.VMEM((bins, width, tile), bf16),
            pltpu.VMEM((slots, tile, width), bf16),
            pltpu.VMEM((slots, tile, width), bf16),
            pltpu.VMEM((2, bins, tile, tile), bf16),
            pltpu.VMEM((bins, tile, tile), f32),
            pltpu.VMEM((width, tile), bf16),
            pltpu.VMEM((width, tile), bf16),
            pltpu.VMEM((tile, width), f32),
            pltpu.VMEM((width, tile), f32),
            pltpu.SemaphoreType.DMA((slots, 2)),
            pltpu.SemaphoreType.DMA((2,)),
        ],
        compiler_params=pltpu.CompilerParams(vmem_limit_bytes=48 * 1024 * 1024),
        cost_estimate=pl.CostEstimate(
            flops=6 * 8 * 64 * 128**3, bytes_accessed=20 * 2**20, transcendentals=8 * 2**20
        ),
    )(place, count, bin_bias, wide.T, wide, *left_from, *right_from, teacher)


AXES = ("z", "core", "y", "x")
TILES_DEV = 4


def own_spot(info, s, slot):
    row = info[s, 2 * slot]
    col = info[s, 2 * slot + 1]
    return (
        (lax.rem(row // 16, 4), lax.rem(row // 4, 4), lax.rem(row, 4)),
        (lax.rem(col // 128, 4), lax.rem(col // 64, 2), lax.rem(col, 4)),
    )


def pick_kernel(info, here, near0, near1, near2, near3, out0, out1, out2, out3, bank):
    outs = (out0, out1, out2, out3)
    for n, near in enumerate((near0, near1, near2, near3)):
        bank[pl.ds(4 * n, 4)] = near[...]
    slots = out0.shape[0]
    for s in range(4):
        for slot in range(slots):
            (_, x, t), _ = own_spot(info, s, slot)
            spot = lax.rem(here[3] - x + 4, 4) * 4 + t
            outs[(4 - s) % 4][slot] = bank[spot]


def pick_tiles(info, here, near):
    slots = (info.shape[1] - 1) // 2
    _, tile, width = near[0].shape
    smem = pl.BlockSpec(memory_space=pltpu.SMEM)
    vmem = pl.BlockSpec(memory_space=pltpu.VMEM)
    return pl.pallas_call(
        pick_kernel,
        out_shape=[jax.ShapeDtypeStruct((slots, tile, width), near[0].dtype)] * 4,
        in_specs=[smem] * 2 + [vmem] * 4,
        out_specs=[vmem] * 4,
        scratch_shapes=[pltpu.VMEM((16, tile, width), near[0].dtype)],
        compiler_params=pltpu.CompilerParams(vmem_limit_bytes=16 * 1024 * 1024),
    )(info, here, *near)


def fold_kernel(side, count, info, here, *refs):
    sources, rows = refs[:count], refs[count : count + 4]
    own, far1, far2, far3, product, total = refs[count + 4 :]
    total[...] = jnp.zeros(total.shape, jnp.float32)
    slots, tile, width = sources[0].shape
    for s, source in enumerate(sources):
        live = info[s, 2 * slots]
        for slot in range(slots):
            (y, x, t), (z, core, u) = own_spot(info, s, slot)
            if side == 0:
                mine, spot = y == here[2], lax.rem(x - here[3] + 4, 4) * 4 + t
            else:
                mine, spot = core == here[1], lax.rem(z - here[0] + 4, 4) * 4 + u

            @pl.when((slot < live) & mine)
            def _():
                total[spot] += source[slot].astype(jnp.float32)

    own[...] = total[pl.ds(0, 4)]
    for n, far in enumerate((far1, far2, far3)):
        far[...] = total[pl.ds(4 * n + 4, 4)].astype(jnp.bfloat16)
    result = jnp.zeros(product.shape, jnp.float32)
    for n in range(4):
        value = total[pl.ds(4 * n, 4)].reshape(4 * tile, width)
        high = value.astype(jnp.bfloat16)
        low = (value - high.astype(jnp.float32)).astype(jnp.bfloat16)
        for part in (high, low):
            result = result + lax.dot_general(
                rows[n][...],
                part,
                (((0,), (0,)), ((), ())),
                preferred_element_type=jnp.float32,
            )
    product[...] = result


def fold_slots(side, info, here, sources, rows):
    _, tile, width = sources[0].shape
    smem = pl.BlockSpec(memory_space=pltpu.SMEM)
    vmem = pl.BlockSpec(memory_space=pltpu.VMEM)
    far = jax.ShapeDtypeStruct((4, tile, width), jnp.bfloat16)
    return pl.pallas_call(
        functools.partial(fold_kernel, side, len(sources)),
        out_shape=[jax.ShapeDtypeStruct((4, tile, width), jnp.float32)]
        + [far] * 3
        + [jax.ShapeDtypeStruct((rows[0].shape[1], width), jnp.float32)],
        in_specs=[smem] * 2 + [vmem] * (len(sources) + 4),
        out_specs=[vmem] * 5,
        scratch_shapes=[pltpu.VMEM((16, tile, width), jnp.float32)],
        compiler_params=pltpu.CompilerParams(vmem_limit_bytes=24 * 1024 * 1024),
    )(info, here, *sources, *rows)


def shift(value, axis, step):
    size = lax.axis_size(axis)
    return lax.ppermute(value, axis, [(i, (i + step) % size) for i in range(size)])


def ring(value, axis):
    return [shift(value, axis, s) for s in range(1, lax.axis_size(axis))]


def after(value, *others):
    return lax.optimization_barrier((value,) + others)[0]


def cut_kernel(here, one, two, own, far1, far2, far3):
    rows = own.shape[0]
    for n, out in enumerate((own, far1, far2, far3)):
        spot = pl.ds(pl.multiple_of(lax.rem(here[0] + n, 4) * rows, 8), rows)
        out[...] = one[spot, :] + two[spot, :]


def paste_kernel(here, part0, part1, part2, part3, out):
    rows = part0.shape[0]
    for n, part in enumerate((part0, part1, part2, part3)):
        spot = pl.ds(pl.multiple_of(lax.rem(here[0] - n + 4, 4) * rows, 8), rows)
        out[spot, :] = part[...]


def small_call(kernel, here, values, outs):
    smem = pl.BlockSpec(memory_space=pltpu.SMEM)
    vmem = pl.BlockSpec(memory_space=pltpu.VMEM)
    return pl.pallas_call(
        kernel,
        out_shape=[jax.ShapeDtypeStruct(shape, jnp.float32) for shape in outs],
        in_specs=[smem] + [vmem] * len(values),
        out_specs=[vmem] * len(outs),
    )(here, *values)


def sum_everywhere(here, mine, other, in_z_step, in_y_step):
    rows, width = mine.shape
    part = (rows // 4, width)
    own, *far = small_call(cut_kernel, here, [mine, shift(other, "core", 1)], [part] * 4)
    in_z_step = after(in_z_step, own)
    for s in (1, 2, 3):
        own = own + shift(far[s - 1], "z", s)
    in_y_step = after(in_y_step, own)
    for axis in ("y", "x"):
        sent = ring(own, axis)
        own = own + sent[0] + sent[1] + sent[2]
    total = small_call(paste_kernel, here, [own] + ring(own, "z"), [(rows, width)])[0]
    return total, in_z_step, in_y_step


def per_device(
    single, left_weight, right_weight, bin_weight, bin_bias, block_tiles, block_count, teacher
):
    slots, bins, tile = teacher.shape[1:4]
    devices = lax.axis_size(AXES)
    own_tiles = block_tiles[0]
    left_wide = left_weight.astype(jnp.float32)
    right_wide = right_weight.astype(jnp.float32)
    info = jnp.concatenate([own_tiles.reshape(1, -1), block_count[None]], axis=1)
    left_local = jnp.dot(single, left_weight, preferred_element_type=jnp.float32).astype(
        jnp.bfloat16
    )
    right_local = jnp.dot(after(single, left_local), right_weight, preferred_element_type=jnp.float32).astype(
        jnp.bfloat16
    )
    rows_dev, width = left_local.shape
    left_local = left_local.reshape(-1, tile, width)
    right_local = right_local.reshape(-1, tile, width)
    here = jnp.stack([lax.axis_index(a) for a in AXES]).astype(jnp.int32)
    z, core, y = here[0], here[1], here[2]
    left_near = [left_local] + ring(left_local, "x")
    right_ring = ring(right_local, "z")
    left_near = after(left_near, *right_ring)
    info_first = after(info, right_local)
    info_y = jnp.concatenate([info_first] + ring(info_first, "y"))
    picked = pick_tiles(info_y, here, left_near)
    left_from = [picked[0]] + [shift(picked[s], "y", s) for s in (1, 2, 3)]
    right_near = jnp.concatenate([right_local] + right_ring)
    right_from = [right_near, shift(right_near, "core", 1)]
    near_x = shift(after(single, right_from[1]), "x", 3)
    left_from[0] = after(picked[0], near_x)
    single_x = after(single, near_x)
    single_z = after(single, right_near)
    rows_x = [single, near_x] + [shift(single_x, "x", 4 - s) for s in (2, 3)]
    rows_z = [single] + [shift(single_z, "z", 4 - s) for s in (1, 2, 3)]
    row, col = own_tiles[:, 0], own_tiles[:, 1]
    place = jnp.stack(
        [
            (y - row // 16 % 4) % 4,
            (core - col // 64 % 2) % 2,
            (z - col // 128 % 4) % 4 * TILES_DEV + col % TILES_DEV,
        ],
        axis=1,
    )
    left_slots, right_slots, bins_part, cross_part = run_blocks(
        place, block_count, bin_weight, bin_bias, left_from, right_from, teacher[0]
    )
    left_slots, right_slots = after((left_slots, right_slots), *rows_x, *rows_z)
    left_ring = ring(left_slots, "y")
    right_slots = after(right_slots, left_ring[0])
    info_last = after(info, right_slots)
    info_core = jnp.concatenate([info_last] + ring(info_last, "core"))
    right_own, *right_far, part_right = fold_slots(
        1, info_core, here, [right_slots] + ring(right_slots, "core"), rows_z
    )
    left_own, *left_far, part_left = fold_slots(
        0, info_y, here, [left_slots] + left_ring, rows_x
    )
    depth = part_left.shape[0]
    scalars = jnp.stack([jnp.sum(cross_part), block_count[0].astype(jnp.float32)])
    part_bin = jnp.sum(bins_part, axis=1)
    first = jnp.concatenate([part_left, part_bin])
    second = jnp.concatenate(
        [part_right, jnp.pad(scalars[None], ((0, bins - 1), (0, width - 2)))]
    )
    low_core = core == 0
    total, left_far, right_far = sum_everywhere(
        here,
        jnp.where(low_core, first, second),
        jnp.where(low_core, second, first),
        left_far,
        right_far,
    )
    left_rows_grad, right_rows_grad = left_own, right_own
    for s in (1, 2, 3):
        left_rows_grad = left_rows_grad + shift(left_far[s - 1], "x", s).astype(jnp.float32)
        right_rows_grad = right_rows_grad + shift(right_far[s - 1], "z", s).astype(jnp.float32)
    left_rows_grad = left_rows_grad.reshape(rows_dev, width)
    right_rows_grad = right_rows_grad.reshape(rows_dev, width)
    other = shift(total, "core", 1)
    first = jnp.where(low_core, total, other)
    second = jnp.where(low_core, other, total)
    grad_single = (
        jnp.dot(left_rows_grad, left_wide.T, precision=lax.Precision.HIGHEST)
        + jnp.dot(right_rows_grad, right_wide.T, precision=lax.Precision.HIGHEST)
    ).astype(jnp.bfloat16)
    grad_left = first[:depth] / devices
    grad_right = second[:depth] / devices
    grad_bin = first[depth : depth + bins].T / devices
    loss_value = second[depth, 0] / (second[depth, 1] * (tile * tile))
    return (grad_single, grad_left, grad_right, grad_bin, loss_value)


def solution(mesh):
    torus = Mesh(mesh.devices.reshape(4, 2, 4, 4), AXES)
    return jax.shard_map(
        per_device,
        mesh=torus,
        in_specs=(
            P(AXES, None),
            P(),
            P(),
            P(),
            P(),
            P(AXES, None, None),
            P(AXES),
            P(AXES, None, None, None, None),
        ),
        out_specs=(P(AXES, None), P(), P(), P(), P()),
        check_vma=False,
    )
```

```python
import functools
import jax
import jax.numpy as jnp
from jax import lax
from jax.experimental import pallas as pl
from jax.experimental.pallas import tpu as pltpu
from jax.sharding import Mesh
from jax.sharding import PartitionSpec as P

GROUP_SCORES = 32
GROUP_SOFT = 16
GROUP_GRADS = 32


def blocks_kernel(
    place, count, bias, w_turned, w_plain, left0, left1, left2, left3, right0, right1,
    right2, right3, teacher,
    left_grads, right_grads, bin_out, cross_out,
    w_rows, w_wide, w_cols, left_tiles, right_tiles, target, logit, left_turn, right_turn, left_sum, right_sum,
    tile_sem, target_sem,
):
    left_from = (left0, left1, left2, left3)
    right_from = (right0, right1, right2, right3)
    slots, bins, tile, width = teacher.shape
    live = count[0]

    def target_copy(slot):
        return pltpu.make_async_copy(
            teacher.at[slot], target.at[lax.rem(slot, 2)], target_sem.at[lax.rem(slot, 2)]
        )

    def left_copy(slot, n):
        return pltpu.make_async_copy(
            left_from[n].at[slot], left_tiles.at[slot], tile_sem.at[slot, 0]
        )

    def right_copy(slot, n):
        return pltpu.make_async_copy(
            right_from[n].at[place[slot, 2]], right_tiles.at[slot], tile_sem.at[slot, 1]
        )

    for slot in range(slots):
        for n in range(len(left_from)):

            @pl.when((slot < live) & (place[slot, 0] == n))
            def _():
                left_copy(slot, n).start()

        for n in range(len(right_from)):

            @pl.when((slot < live) & (place[slot, 1] == n))
            def _():
                right_copy(slot, n).start()

    target_copy(0).start()
    for k in range(bins):
        row = w_turned[k : k + 1, :]
        w_wide[k] = jnp.broadcast_to(row, (8, width))
        w_rows[k] = jnp.broadcast_to(row, (16, width)).astype(jnp.bfloat16)
        w_cols[k] = jnp.broadcast_to(w_plain[:, k : k + 1], (width, tile)).astype(jnp.bfloat16)
    bin_out[...] = jnp.zeros(bin_out.shape, jnp.float32)
    cross_out[...] = jnp.zeros(cross_out.shape, jnp.float32)

    def block(slot, _):
        buf = lax.rem(slot, 2)

        @pl.when(slot + 1 < live)
        def _():
            target_copy(slot + 1).start()

        left_copy(slot, 0).wait()
        right_copy(slot, 0).wait()
        left = left_tiles[slot]
        right = right_tiles[slot]
        left_turn[...] = left.T
        right_turn[...] = right.T
        left_sum[...] = jnp.zeros(left_sum.shape, jnp.float32)
        right_sum[...] = jnp.zeros(right_sum.shape, jnp.float32)

        def scores(g, highest):
            left = left_tiles[slot].reshape(tile // 16, 16, width)
            for j in range(GROUP_SCORES):
                k = g * GROUP_SCORES + j
                scaled = (left * w_rows[k][None]).reshape(tile, width)
                value = jnp.dot(scaled, right_turn[...], preferred_element_type=jnp.float32)
                value = value + bias[k]
                logit[k] = value
                highest = jnp.maximum(highest, value)
            return highest

        highest = lax.fori_loop(
            0, bins // GROUP_SCORES, scores, jnp.full((tile, tile), -jnp.inf, jnp.float32)
        )
        target_copy(slot).wait()

        STEP = 32
        ratios = []
        for p in range(0, tile, STEP):
            rows = pl.ds(p, STEP)
            top = highest[p : p + STEP]

            def soft(g, carried):
                total, mass, cross = carried
                for j in range(GROUP_SOFT):
                    k = g * GROUP_SOFT + j
                    value = logit[k, rows, :] - top
                    power = jnp.exp(value)
                    goal = target[buf, k, rows, :].astype(jnp.float32)
                    total = total + power
                    mass = mass + goal
                    cross = cross + goal * value
                    logit[k, rows, :] = power
                return total, mass, cross

            zero = jnp.zeros((STEP, tile), jnp.float32)
            total, mass, cross = lax.fori_loop(0, bins // GROUP_SOFT, soft, (zero, zero, zero))
            cross = mass * jnp.log(total) - cross
            cross_out[...] += cross.reshape(STEP // 8, 8, tile).sum(0)
            ratios.append(mass / total)
        ratio = jnp.concatenate(ratios, 0)

        def grads(g, _):
            left_wide = left_tiles[slot].astype(jnp.float32)
            pieces, scales = [], []
            left_part = jnp.zeros((tile, width), jnp.float32)
            for j in range(GROUP_GRADS):
                k = g * GROUP_GRADS + j
                grad = logit[k] * ratio - target[buf, k].astype(jnp.float32)
                grad = grad.astype(jnp.bfloat16)
                mixed = jnp.dot(grad, right_tiles[slot], preferred_element_type=jnp.float32)
                left_part = left_part + (
                    mixed.reshape(tile // 8, 8, width) * w_wide[k][None]
                ).reshape(tile, width)
                bin_out[k] += (mixed * left_wide).reshape(tile // 8, 8, width).sum(0)
                pieces.append(grad)
                scales.append(left_turn[...] * w_cols[k])
            left_sum[...] += left_part
            right_sum[...] += jnp.dot(
                jnp.concatenate(scales, 1),
                jnp.concatenate(pieces, 0),
                preferred_element_type=jnp.float32,
            )
            return 0

        lax.fori_loop(0, bins // GROUP_GRADS, grads, 0)
        left_grads[slot] = left_sum[...].astype(jnp.bfloat16)
        right_grads[slot] = right_sum[...].T.astype(jnp.bfloat16)
        return 0

    lax.fori_loop(0, live, block, 0)


def run_blocks(place, count, bin_weight, bin_bias, left_from, right_from, teacher):
    slots, bins, tile, _ = teacher.shape
    width = bin_weight.shape[0]
    wide = bin_weight.astype(jnp.float32)
    smem = pl.BlockSpec(memory_space=pltpu.SMEM)
    vmem = pl.BlockSpec(memory_space=pltpu.VMEM)
    hbm = pl.BlockSpec(memory_space=pl.ANY)
    f32, bf16 = jnp.float32, jnp.bfloat16
    piece = jax.ShapeDtypeStruct((slots, tile, width), bf16)
    return pl.pallas_call(
        blocks_kernel,
        out_shape=[piece] * 2
        + [
            jax.ShapeDtypeStruct((bins, 8, width), f32),
            jax.ShapeDtypeStruct((8, tile), f32),
        ],
        in_specs=[smem] * 3 + [vmem] * 2 + [hbm] * 9,
        out_specs=[vmem] * 4,
        scratch_shapes=[
            pltpu.VMEM((bins, 16, width), bf16),
            pltpu.VMEM((bins, 8, width), f32),
            pltpu.VMEM((bins, width, tile), bf16),
            pltpu.VMEM((slots, tile, width), bf16),
            pltpu.VMEM((slots, tile, width), bf16),
            pltpu.VMEM((2, bins, tile, tile), bf16),
            pltpu.VMEM((bins, tile, tile), f32),
            pltpu.VMEM((width, tile), bf16),
            pltpu.VMEM((width, tile), bf16),
            pltpu.VMEM((tile, width), f32),
            pltpu.VMEM((width, tile), f32),
            pltpu.SemaphoreType.DMA((slots, 2)),
            pltpu.SemaphoreType.DMA((2,)),
        ],
        compiler_params=pltpu.CompilerParams(vmem_limit_bytes=48 * 1024 * 1024),
        cost_estimate=pl.CostEstimate(
            flops=6 * 8 * 64 * 128**3, bytes_accessed=20 * 2**20, transcendentals=8 * 2**20
        ),
    )(place, count, bin_bias, wide.T, wide, *left_from, *right_from, teacher)


AXES = ("z", "core", "y", "x")
TILES_DEV = 4


def own_spot(info, s, slot):
    row = info[s, 2 * slot]
    col = info[s, 2 * slot + 1]
    return (
        (lax.rem(row // 16, 4), lax.rem(row // 4, 4), lax.rem(row, 4)),
        (lax.rem(col // 128, 4), lax.rem(col // 64, 2), lax.rem(col, 4)),
    )


def pick_kernel(info, here, near0, near1, near2, near3, out0, out1, out2, out3, bank):
    outs = (out0, out1, out2, out3)
    for n, near in enumerate((near0, near1, near2, near3)):
        bank[pl.ds(4 * n, 4)] = near[...]
    slots = out0.shape[0]
    for s in range(4):
        for slot in range(slots):
            (_, x, t), _ = own_spot(info, s, slot)
            spot = lax.rem(here[3] - x + 4, 4) * 4 + t
            outs[(4 - s) % 4][slot] = bank[spot]


def pick_tiles(info, here, near):
    slots = (info.shape[1] - 1) // 2
    _, tile, width = near[0].shape
    smem = pl.BlockSpec(memory_space=pltpu.SMEM)
    vmem = pl.BlockSpec(memory_space=pltpu.VMEM)
    return pl.pallas_call(
        pick_kernel,
        out_shape=[jax.ShapeDtypeStruct((slots, tile, width), near[0].dtype)] * 4,
        in_specs=[smem] * 2 + [vmem] * 4,
        out_specs=[vmem] * 4,
        scratch_shapes=[pltpu.VMEM((16, tile, width), near[0].dtype)],
        compiler_params=pltpu.CompilerParams(vmem_limit_bytes=16 * 1024 * 1024),
    )(info, here, *near)


def fold_kernel(side, info, here, *refs):
    sources, (own, far1, far2, far3, total) = refs[:-5], refs[-5:]
    total[...] = jnp.zeros(total.shape, jnp.float32)
    slots = sources[0].shape[0]
    for s, source in enumerate(sources):
        live = info[s, 2 * slots]
        for slot in range(slots):
            (y, x, t), (z, core, u) = own_spot(info, s, slot)
            if side == 0:
                mine, spot = y == here[2], lax.rem(x - here[3] + 4, 4) * 4 + t
            else:
                mine, spot = core == here[1], lax.rem(z - here[0] + 4, 4) * 4 + u

            @pl.when((slot < live) & mine)
            def _():
                total[spot] += source[slot].astype(jnp.float32)

    own[...] = total[pl.ds(0, 4)]
    for n, far in enumerate((far1, far2, far3)):
        far[...] = total[pl.ds(4 * n + 4, 4)].astype(jnp.bfloat16)


def fold_slots(side, info, here, sources):
    _, tile, width = sources[0].shape
    smem = pl.BlockSpec(memory_space=pltpu.SMEM)
    vmem = pl.BlockSpec(memory_space=pltpu.VMEM)
    far = jax.ShapeDtypeStruct((4, tile, width), jnp.bfloat16)
    return pl.pallas_call(
        functools.partial(fold_kernel, side),
        out_shape=[jax.ShapeDtypeStruct((4, tile, width), jnp.float32)] + [far] * 3,
        in_specs=[smem] * 2 + [vmem] * len(sources),
        out_specs=[vmem] * 4,
        scratch_shapes=[pltpu.VMEM((16, tile, width), jnp.float32)],
        compiler_params=pltpu.CompilerParams(vmem_limit_bytes=16 * 1024 * 1024),
    )(info, here, *sources)


def shift(value, axis, step):
    size = lax.axis_size(axis)
    return lax.ppermute(value, axis, [(i, (i + step) % size) for i in range(size)])


def ring(value, axis):
    return [shift(value, axis, s) for s in range(1, lax.axis_size(axis))]


def after(value, *others):
    return lax.optimization_barrier((value,) + others)[0]


def low_parts(value, count):
    parts = []
    for _ in range(count):
        parts.append(value.astype(jnp.bfloat16))
        value = value - parts[-1].astype(jnp.float32)
    return parts


def per_device(
    single, left_weight, right_weight, bin_weight, bin_bias, block_tiles, block_count, teacher
):
    slots, bins, tile = teacher.shape[1:4]
    devices = lax.axis_size(AXES)
    own_tiles = block_tiles[0]
    left_wide = left_weight.astype(jnp.float32)
    right_wide = right_weight.astype(jnp.float32)
    info = jnp.concatenate([own_tiles.reshape(1, -1), block_count[None]], axis=1)
    left_local = jnp.dot(single, left_weight, preferred_element_type=jnp.float32).astype(
        jnp.bfloat16
    )
    rows_dev, width = left_local.shape
    left_local = left_local.reshape(-1, tile, width)
    here = jnp.stack([lax.axis_index(a) for a in AXES]).astype(jnp.int32)
    z, core, y = here[0], here[1], here[2]
    left_near = [left_local] + ring(left_local, "x")
    info_first = after(info, left_local)
    right_local = jnp.dot(after(single, left_near[1]), right_weight, preferred_element_type=jnp.float32).astype(
        jnp.bfloat16
    )
    right_local = right_local.reshape(-1, tile, width)
    info_y = jnp.concatenate([info_first] + ring(info_first, "y"))
    picked = pick_tiles(info_y, here, left_near)
    left_from = [picked[0]] + [shift(picked[s], "y", s) for s in (1, 2, 3)]
    right_pair = jnp.concatenate([right_local, shift(right_local, "core", 1)])
    right_pair = after(right_pair, *picked)
    right_from = [right_pair] + ring(right_pair, "z")
    row, col = own_tiles[:, 0], own_tiles[:, 1]
    place = jnp.stack(
        [
            (y - row // 16 % 4) % 4,
            (z - col // 128 % 4) % 4,
            (core - col // 64 % 2) % 2 * TILES_DEV + col % TILES_DEV,
        ],
        axis=1,
    )
    left_slots, right_slots, bins_part, cross_part = run_blocks(
        place, block_count, bin_weight, bin_bias, left_from, right_from, teacher[0]
    )
    left_ring = ring(left_slots, "y")
    info_last = after(info, right_slots)
    info_core = jnp.concatenate([info_last] + ring(info_last, "core"))
    right_ring = ring(right_slots, "core")
    left_own, *left_far = fold_slots(0, info_y, here, [left_slots] + left_ring)
    right_own, *right_far = fold_slots(1, info_core, here, [right_slots] + right_ring)
    left_rows_grad, right_rows_grad = left_own, right_own
    for s in (1, 2, 3):
        left_rows_grad = left_rows_grad + shift(left_far[s - 1], "x", s).astype(jnp.float32)
        right_rows_grad = right_rows_grad + shift(right_far[s - 1], "z", s).astype(jnp.float32)
    left_rows_grad = left_rows_grad.reshape(rows_dev, width)
    right_rows_grad = right_rows_grad.reshape(rows_dev, width)
    single_wide = single.astype(jnp.float32)
    part_left = jnp.dot(single_wide.T, left_rows_grad, precision=lax.Precision.HIGHEST)
    part_right = jnp.dot(single_wide.T, right_rows_grad, precision=lax.Precision.HIGHEST)
    depth = part_left.shape[0]
    rows_sum = 2 * depth + bins
    chunk = rows_sum // devices + 1
    last = rows_sum // chunk, rows_sum % chunk
    bf16, f32 = jnp.bfloat16, jnp.float32
    scalars = jnp.stack(low_parts(jnp.sum(cross_part), 3) + [block_count[0].astype(bf16)])
    packed = jnp.concatenate(
        [
            part_left.astype(bf16),
            part_right.astype(bf16),
            jnp.sum(bins_part, axis=1).astype(bf16),
            jnp.pad(scalars[None], ((0, chunk * devices - rows_sum - 1), (0, width - 4))),
        ]
    ).reshape(devices, chunk, width)
    mine = jnp.sum(lax.all_to_all(packed, AXES, 0, 0).astype(f32), axis=0)
    high, low = low_parts(mine, 2)
    mine = jnp.concatenate([high, low[last[1] : last[1] + 1]])
    totals = lax.all_to_all(
        jnp.broadcast_to(mine[None], (devices, chunk + 1, width)), AXES, 0, 0
    ).astype(f32)
    scalars = totals[last[0], last[1]] + totals[last[0], chunk]
    totals = totals[:, :chunk].reshape(-1, width)
    grad_single = (
        jnp.dot(left_rows_grad, left_wide.T, precision=lax.Precision.HIGHEST)
        + jnp.dot(right_rows_grad, right_wide.T, precision=lax.Precision.HIGHEST)
    ).astype(jnp.bfloat16)
    grad_left = totals[:depth] / devices
    grad_right = totals[depth : 2 * depth] / devices
    grad_bin = totals[2 * depth : rows_sum].T / devices
    cross_total = scalars[0] + scalars[1] + scalars[2]
    loss_value = cross_total / (scalars[3] * (tile * tile))
    return (grad_single, grad_left, grad_right, grad_bin, loss_value)


def solution(mesh):
    torus = Mesh(mesh.devices.reshape(4, 2, 4, 4), AXES)
    return jax.shard_map(
        per_device,
        mesh=torus,
        in_specs=(
            P(AXES, None),
            P(),
            P(),
            P(),
            P(),
            P(AXES, None, None),
            P(AXES),
            P(AXES, None, None, None, None),
        ),
        out_specs=(P(AXES, None), P(), P(), P(), P()),
        check_vma=False,
    )
```

```python
import functools
import jax
import jax.numpy as jnp
from jax import lax
from jax.experimental import pallas as pl
from jax.experimental.pallas import tpu as pltpu
from jax.sharding import Mesh
from jax.sharding import PartitionSpec as P

GROUP_SCORES = 32
GROUP_SOFT = 16
GROUP_GRADS = 32


def blocks_kernel(
    place, count, bias, w_turned, w_plain, left0, left1, left2, left3, right0, right1,
    right2, right3, teacher,
    left_grads, right_grads, bin_out, cross_out,
    w_rows, w_wide, w_cols, left_tiles, right_tiles, target, logit, left_turn, right_turn, left_sum, right_sum,
    tile_sem, target_sem,
):
    left_from = (left0, left1, left2, left3)
    right_from = (right0, right1, right2, right3)
    slots, bins, tile, width = teacher.shape
    live = count[0]

    def target_copy(slot):
        return pltpu.make_async_copy(
            teacher.at[slot], target.at[lax.rem(slot, 2)], target_sem.at[lax.rem(slot, 2)]
        )

    def left_copy(slot, n):
        return pltpu.make_async_copy(
            left_from[n].at[slot], left_tiles.at[slot], tile_sem.at[slot, 0]
        )

    def right_copy(slot, n):
        return pltpu.make_async_copy(
            right_from[n].at[place[slot, 2]], right_tiles.at[slot], tile_sem.at[slot, 1]
        )

    for slot in range(slots):
        for n in range(len(left_from)):

            @pl.when((slot < live) & (place[slot, 0] == n))
            def _():
                left_copy(slot, n).start()

        for n in range(len(right_from)):

            @pl.when((slot < live) & (place[slot, 1] == n))
            def _():
                right_copy(slot, n).start()

    target_copy(0).start()
    for k in range(bins):
        row = w_turned[k : k + 1, :]
        w_wide[k] = jnp.broadcast_to(row, (8, width))
        w_rows[k] = jnp.broadcast_to(row, (16, width)).astype(jnp.bfloat16)
        w_cols[k] = jnp.broadcast_to(w_plain[:, k : k + 1], (width, tile)).astype(jnp.bfloat16)
    bin_out[...] = jnp.zeros(bin_out.shape, jnp.float32)
    cross_out[...] = jnp.zeros(cross_out.shape, jnp.float32)

    def block(slot, _):
        buf = lax.rem(slot, 2)

        @pl.when(slot + 1 < live)
        def _():
            target_copy(slot + 1).start()

        left_copy(slot, 0).wait()
        right_copy(slot, 0).wait()
        left = left_tiles[slot]
        right = right_tiles[slot]
        left_turn[...] = left.T
        right_turn[...] = right.T
        left_sum[...] = jnp.zeros(left_sum.shape, jnp.float32)
        right_sum[...] = jnp.zeros(right_sum.shape, jnp.float32)

        def scores(g, highest):
            left = left_tiles[slot].reshape(tile // 16, 16, width)
            for j in range(GROUP_SCORES):
                k = g * GROUP_SCORES + j
                scaled = (left * w_rows[k][None]).reshape(tile, width)
                value = jnp.dot(scaled, right_turn[...], preferred_element_type=jnp.float32)
                value = value + bias[k]
                logit[k] = value
                highest = jnp.maximum(highest, value)
            return highest

        highest = lax.fori_loop(
            0, bins // GROUP_SCORES, scores, jnp.full((tile, tile), -jnp.inf, jnp.float32)
        )
        target_copy(slot).wait()

        STEP = 32
        ratios = []
        for p in range(0, tile, STEP):
            rows = pl.ds(p, STEP)
            top = highest[p : p + STEP]

            def soft(g, carried):
                total, mass, cross = carried
                for j in range(GROUP_SOFT):
                    k = g * GROUP_SOFT + j
                    value = logit[k, rows, :] - top
                    power = jnp.exp(value)
                    goal = target[buf, k, rows, :].astype(jnp.float32)
                    total = total + power
                    mass = mass + goal
                    cross = cross + goal * value
                    logit[k, rows, :] = power
                return total, mass, cross

            zero = jnp.zeros((STEP, tile), jnp.float32)
            total, mass, cross = lax.fori_loop(0, bins // GROUP_SOFT, soft, (zero, zero, zero))
            cross = mass * jnp.log(total) - cross
            cross_out[...] += cross.reshape(STEP // 8, 8, tile).sum(0)
            ratios.append(mass / total)
        ratio = jnp.concatenate(ratios, 0)

        def grads(g, _):
            left_wide = left_tiles[slot].astype(jnp.float32)
            pieces, scales = [], []
            left_part = jnp.zeros((tile, width), jnp.float32)
            for j in range(GROUP_GRADS):
                k = g * GROUP_GRADS + j
                grad = logit[k] * ratio - target[buf, k].astype(jnp.float32)
                grad = grad.astype(jnp.bfloat16)
                mixed = jnp.dot(grad, right_tiles[slot], preferred_element_type=jnp.float32)
                left_part = left_part + (
                    mixed.reshape(tile // 8, 8, width) * w_wide[k][None]
                ).reshape(tile, width)
                bin_out[k] += (mixed * left_wide).reshape(tile // 8, 8, width).sum(0)
                pieces.append(grad)
                scales.append(left_turn[...] * w_cols[k])
            left_sum[...] += left_part
            right_sum[...] += jnp.dot(
                jnp.concatenate(scales, 1),
                jnp.concatenate(pieces, 0),
                preferred_element_type=jnp.float32,
            )
            return 0

        lax.fori_loop(0, bins // GROUP_GRADS, grads, 0)
        left_grads[slot] = left_sum[...].astype(jnp.bfloat16)
        right_grads[slot] = right_sum[...].T.astype(jnp.bfloat16)
        return 0

    lax.fori_loop(0, live, block, 0)


def run_blocks(place, count, bin_weight, bin_bias, left_from, right_from, teacher):
    slots, bins, tile, _ = teacher.shape
    width = bin_weight.shape[0]
    wide = bin_weight.astype(jnp.float32)
    smem = pl.BlockSpec(memory_space=pltpu.SMEM)
    vmem = pl.BlockSpec(memory_space=pltpu.VMEM)
    hbm = pl.BlockSpec(memory_space=pl.ANY)
    f32, bf16 = jnp.float32, jnp.bfloat16
    piece = jax.ShapeDtypeStruct((slots, tile, width), bf16)
    return pl.pallas_call(
        blocks_kernel,
        out_shape=[piece] * 2
        + [
            jax.ShapeDtypeStruct((bins, 8, width), f32),
            jax.ShapeDtypeStruct((8, tile), f32),
        ],
        in_specs=[smem] * 3 + [vmem] * 2 + [hbm] * 9,
        out_specs=[vmem] * 4,
        scratch_shapes=[
            pltpu.VMEM((bins, 16, width), bf16),
            pltpu.VMEM((bins, 8, width), f32),
            pltpu.VMEM((bins, width, tile), bf16),
            pltpu.VMEM((slots, tile, width), bf16),
            pltpu.VMEM((slots, tile, width), bf16),
            pltpu.VMEM((2, bins, tile, tile), bf16),
            pltpu.VMEM((bins, tile, tile), f32),
            pltpu.VMEM((width, tile), bf16),
            pltpu.VMEM((width, tile), bf16),
            pltpu.VMEM((tile, width), f32),
            pltpu.VMEM((width, tile), f32),
            pltpu.SemaphoreType.DMA((slots, 2)),
            pltpu.SemaphoreType.DMA((2,)),
        ],
        compiler_params=pltpu.CompilerParams(vmem_limit_bytes=48 * 1024 * 1024),
        cost_estimate=pl.CostEstimate(
            flops=6 * 8 * 64 * 128**3, bytes_accessed=20 * 2**20, transcendentals=8 * 2**20
        ),
    )(place, count, bin_bias, wide.T, wide, *left_from, *right_from, teacher)


AXES = ("z", "core", "y", "x")
TILES_DEV = 4


def own_spot(info, s, slot):
    row = info[s, 2 * slot]
    col = info[s, 2 * slot + 1]
    return (
        (lax.rem(row // 16, 4), lax.rem(row // 4, 4), lax.rem(row, 4)),
        (lax.rem(col // 128, 4), lax.rem(col // 64, 2), lax.rem(col, 4)),
    )


def pick_kernel(info, here, near0, near1, near2, near3, out0, out1, out2, out3, bank):
    outs = (out0, out1, out2, out3)
    for n, near in enumerate((near0, near1, near2, near3)):
        bank[pl.ds(4 * n, 4)] = near[...]
    slots = out0.shape[0]
    for s in range(4):
        for slot in range(slots):
            (_, x, t), _ = own_spot(info, s, slot)
            spot = lax.rem(here[3] - x + 4, 4) * 4 + t
            outs[(4 - s) % 4][slot] = bank[spot]


def pick_tiles(info, here, near):
    slots = (info.shape[1] - 1) // 2
    _, tile, width = near[0].shape
    smem = pl.BlockSpec(memory_space=pltpu.SMEM)
    vmem = pl.BlockSpec(memory_space=pltpu.VMEM)
    return pl.pallas_call(
        pick_kernel,
        out_shape=[jax.ShapeDtypeStruct((slots, tile, width), near[0].dtype)] * 4,
        in_specs=[smem] * 2 + [vmem] * 4,
        out_specs=[vmem] * 4,
        scratch_shapes=[pltpu.VMEM((16, tile, width), near[0].dtype)],
        compiler_params=pltpu.CompilerParams(vmem_limit_bytes=16 * 1024 * 1024),
    )(info, here, *near)


def fold_kernel(side, info, here, *refs):
    sources, (own, far1, far2, far3, total) = refs[:-5], refs[-5:]
    total[...] = jnp.zeros(total.shape, jnp.float32)
    slots = sources[0].shape[0]
    for s, source in enumerate(sources):
        live = info[s, 2 * slots]
        for slot in range(slots):
            (y, x, t), (z, core, u) = own_spot(info, s, slot)
            if side == 0:
                mine, spot = y == here[2], lax.rem(x - here[3] + 4, 4) * 4 + t
            else:
                mine, spot = core == here[1], lax.rem(z - here[0] + 4, 4) * 4 + u

            @pl.when((slot < live) & mine)
            def _():
                total[spot] += source[slot].astype(jnp.float32)

    own[...] = total[pl.ds(0, 4)]
    for n, far in enumerate((far1, far2, far3)):
        far[...] = total[pl.ds(4 * n + 4, 4)].astype(jnp.bfloat16)


def fold_slots(side, info, here, sources):
    _, tile, width = sources[0].shape
    smem = pl.BlockSpec(memory_space=pltpu.SMEM)
    vmem = pl.BlockSpec(memory_space=pltpu.VMEM)
    far = jax.ShapeDtypeStruct((4, tile, width), jnp.bfloat16)
    return pl.pallas_call(
        functools.partial(fold_kernel, side),
        out_shape=[jax.ShapeDtypeStruct((4, tile, width), jnp.float32)] + [far] * 3,
        in_specs=[smem] * 2 + [vmem] * len(sources),
        out_specs=[vmem] * 4,
        scratch_shapes=[pltpu.VMEM((16, tile, width), jnp.float32)],
        compiler_params=pltpu.CompilerParams(vmem_limit_bytes=16 * 1024 * 1024),
    )(info, here, *sources)


def shift(value, axis, step):
    size = lax.axis_size(axis)
    return lax.ppermute(value, axis, [(i, (i + step) % size) for i in range(size)])


def ring(value, axis):
    return [shift(value, axis, s) for s in range(1, lax.axis_size(axis))]


def after(value, *others):
    return lax.optimization_barrier((value,) + others)[0]


def low_parts(value, count):
    parts = []
    for _ in range(count):
        parts.append(value.astype(jnp.bfloat16))
        value = value - parts[-1].astype(jnp.float32)
    return parts


def per_device(
    single, left_weight, right_weight, bin_weight, bin_bias, block_tiles, block_count, teacher
):
    slots, bins, tile = teacher.shape[1:4]
    devices = lax.axis_size(AXES)
    own_tiles = block_tiles[0]
    left_wide = left_weight.astype(jnp.float32)
    right_wide = right_weight.astype(jnp.float32)
    info = jnp.concatenate([own_tiles.reshape(1, -1), block_count[None]], axis=1)
    left_local = jnp.dot(single, left_weight, preferred_element_type=jnp.float32).astype(
        jnp.bfloat16
    )
    rows_dev, width = left_local.shape
    left_local = left_local.reshape(-1, tile, width)
    here = jnp.stack([lax.axis_index(a) for a in AXES]).astype(jnp.int32)
    z, core, y = here[0], here[1], here[2]
    left_near = [left_local] + ring(left_local, "x")
    info_first = after(info, left_local)
    right_local = jnp.dot(after(single, left_near[1]), right_weight, preferred_element_type=jnp.float32).astype(
        jnp.bfloat16
    )
    right_local = right_local.reshape(-1, tile, width)
    info_y = jnp.concatenate([info_first] + ring(info_first, "y"))
    picked = pick_tiles(info_y, here, left_near)
    left_from = [picked[0]] + [shift(picked[s], "y", s) for s in (1, 2, 3)]
    right_pair = jnp.concatenate([right_local, shift(right_local, "core", 1)])
    right_pair = after(right_pair, *picked)
    right_from = [right_pair] + ring(right_pair, "z")
    row, col = own_tiles[:, 0], own_tiles[:, 1]
    place = jnp.stack(
        [
            (y - row // 16 % 4) % 4,
            (z - col // 128 % 4) % 4,
            (core - col // 64 % 2) % 2 * TILES_DEV + col % TILES_DEV,
        ],
        axis=1,
    )
    info_last = after(info, *picked)
    info_core = jnp.concatenate([info_last] + ring(info_last, "core"))
    place = after(place, info_core)
    left_slots, right_slots, bins_part, cross_part = run_blocks(
        place, block_count, bin_weight, bin_bias, left_from, right_from, teacher[0]
    )
    left_ring = ring(left_slots, "y")
    right_ring = ring(right_slots, "core")
    right_rows_grad, *right_far = fold_slots(1, info_core, here, [right_slots] + right_ring)
    right_far = [shift(right_far[s - 1], "z", s) for s in (1, 2, 3)]
    left_ring = after(left_ring, *right_far)
    left_rows_grad, *left_far = fold_slots(0, info_y, here, [left_slots] + left_ring)
    for s in (1, 2, 3):
        left_rows_grad = left_rows_grad + shift(left_far[s - 1], "x", s).astype(jnp.float32)
        right_rows_grad = right_rows_grad + right_far[s - 1].astype(jnp.float32)
    left_rows_grad = left_rows_grad.reshape(rows_dev, width)
    right_rows_grad = right_rows_grad.reshape(rows_dev, width)
    single_wide = single.astype(jnp.float32)
    part_left = jnp.dot(single_wide.T, left_rows_grad, precision=lax.Precision.HIGHEST)
    part_right = jnp.dot(single_wide.T, right_rows_grad, precision=lax.Precision.HIGHEST)
    depth = part_left.shape[0]
    rows_sum = 2 * depth + bins
    chunk = rows_sum // devices + 1
    last = rows_sum // chunk, rows_sum % chunk
    bf16, f32 = jnp.bfloat16, jnp.float32
    scalars = jnp.stack(low_parts(jnp.sum(cross_part), 3) + [block_count[0].astype(bf16)])
    packed = jnp.concatenate(
        [
            part_left.astype(bf16),
            part_right.astype(bf16),
            jnp.sum(bins_part, axis=1).astype(bf16),
            jnp.pad(scalars[None], ((0, chunk * devices - rows_sum - 1), (0, width - 4))),
        ]
    ).reshape(devices, chunk, width)
    mine = jnp.sum(lax.all_to_all(packed, AXES, 0, 0).astype(f32), axis=0)
    high, low = low_parts(mine, 2)
    mine = jnp.concatenate([high, low[last[1] : last[1] + 1]])
    totals = lax.all_to_all(
        jnp.broadcast_to(mine[None], (devices, chunk + 1, width)), AXES, 0, 0
    ).astype(f32)
    scalars = totals[last[0], last[1]] + totals[last[0], chunk]
    totals = totals[:, :chunk].reshape(-1, width)
    grad_single = (
        jnp.dot(left_rows_grad, left_wide.T, precision=lax.Precision.HIGHEST)
        + jnp.dot(right_rows_grad, right_wide.T, precision=lax.Precision.HIGHEST)
    ).astype(jnp.bfloat16)
    grad_left = totals[:depth] / devices
    grad_right = totals[depth : 2 * depth] / devices
    grad_bin = totals[2 * depth : rows_sum].T / devices
    cross_total = scalars[0] + scalars[1] + scalars[2]
    loss_value = cross_total / (scalars[3] * (tile * tile))
    return (grad_single, grad_left, grad_right, grad_bin, loss_value)


def solution(mesh):
    torus = Mesh(mesh.devices.reshape(4, 2, 4, 4), AXES)
    return jax.shard_map(
        per_device,
        mesh=torus,
        in_specs=(
            P(AXES, None),
            P(),
            P(),
            P(),
            P(),
            P(AXES, None, None),
            P(AXES),
            P(AXES, None, None, None, None),
        ),
        out_specs=(P(AXES, None), P(), P(), P(), P()),
        check_vma=False,
    )
```

```python
import functools
import jax
import jax.numpy as jnp
from jax import lax
from jax.experimental import pallas as pl
from jax.experimental.pallas import tpu as pltpu
from jax.sharding import Mesh
from jax.sharding import PartitionSpec as P

GROUP_SCORES = 32
GROUP_SOFT = 16
GROUP_GRADS = 32


def blocks_kernel(
    place, count, bias, w_turned, w_plain, left0, left1, left2, left3, right0, right1,
    right2, right3, teacher,
    left_grads, right_grads, bin_out, cross_out,
    w_rows, w_wide, w_cols, left_tiles, right_tiles, target, logit, left_turn, right_turn, left_sum, right_sum,
    tile_sem, target_sem,
):
    left_from = (left0, left1, left2, left3)
    right_from = (right0, right1, right2, right3)
    slots, bins, tile, width = teacher.shape
    live = count[0]

    def target_copy(slot):
        return pltpu.make_async_copy(
            teacher.at[slot], target.at[lax.rem(slot, 2)], target_sem.at[lax.rem(slot, 2)]
        )

    def left_copy(slot, n):
        return pltpu.make_async_copy(
            left_from[n].at[slot], left_tiles.at[slot], tile_sem.at[slot, 0]
        )

    def right_copy(slot, n):
        return pltpu.make_async_copy(
            right_from[n].at[place[slot, 2]], right_tiles.at[slot], tile_sem.at[slot, 1]
        )

    for slot in range(slots):
        for n in range(len(left_from)):

            @pl.when((slot < live) & (place[slot, 0] == n))
            def _():
                left_copy(slot, n).start()

        for n in range(len(right_from)):

            @pl.when((slot < live) & (place[slot, 1] == n))
            def _():
                right_copy(slot, n).start()

    target_copy(0).start()
    for k in range(bins):
        row = w_turned[k : k + 1, :]
        w_wide[k] = jnp.broadcast_to(row, (8, width))
        w_rows[k] = jnp.broadcast_to(row, (16, width)).astype(jnp.bfloat16)
        w_cols[k] = jnp.broadcast_to(w_plain[:, k : k + 1], (width, tile)).astype(jnp.bfloat16)
    bin_out[...] = jnp.zeros(bin_out.shape, jnp.float32)
    cross_out[...] = jnp.zeros(cross_out.shape, jnp.float32)

    def block(slot, _):
        buf = lax.rem(slot, 2)

        @pl.when(slot + 1 < live)
        def _():
            target_copy(slot + 1).start()

        left_copy(slot, 0).wait()
        right_copy(slot, 0).wait()
        left = left_tiles[slot]
        right = right_tiles[slot]
        left_turn[...] = left.T
        right_turn[...] = right.T
        left_sum[...] = jnp.zeros(left_sum.shape, jnp.float32)
        right_sum[...] = jnp.zeros(right_sum.shape, jnp.float32)

        def scores(g, highest):
            left = left_tiles[slot].reshape(tile // 16, 16, width)
            for j in range(GROUP_SCORES):
                k = g * GROUP_SCORES + j
                scaled = (left * w_rows[k][None]).reshape(tile, width)
                value = jnp.dot(scaled, right_turn[...], preferred_element_type=jnp.float32)
                value = value + bias[k]
                logit[k] = value
                highest = jnp.maximum(highest, value)
            return highest

        highest = lax.fori_loop(
            0, bins // GROUP_SCORES, scores, jnp.full((tile, tile), -jnp.inf, jnp.float32)
        )
        target_copy(slot).wait()

        STEP = 32
        ratios = []
        for p in range(0, tile, STEP):
            rows = pl.ds(p, STEP)
            top = highest[p : p + STEP]

            def soft(g, carried):
                total, mass, cross = carried
                for j in range(GROUP_SOFT):
                    k = g * GROUP_SOFT + j
                    value = logit[k, rows, :] - top
                    power = jnp.exp(value)
                    goal = target[buf, k, rows, :].astype(jnp.float32)
                    total = total + power
                    mass = mass + goal
                    cross = cross + goal * value
                    logit[k, rows, :] = power
                return total, mass, cross

            zero = jnp.zeros((STEP, tile), jnp.float32)
            total, mass, cross = lax.fori_loop(0, bins // GROUP_SOFT, soft, (zero, zero, zero))
            cross = mass * jnp.log(total) - cross
            cross_out[...] += cross.reshape(STEP // 8, 8, tile).sum(0)
            ratios.append(mass / total)
        ratio = jnp.concatenate(ratios, 0)

        def grads(g, _):
            left_wide = left_tiles[slot].astype(jnp.float32)
            pieces, scales = [], []
            left_part = jnp.zeros((tile, width), jnp.float32)
            for j in range(GROUP_GRADS):
                k = g * GROUP_GRADS + j
                grad = logit[k] * ratio - target[buf, k].astype(jnp.float32)
                grad = grad.astype(jnp.bfloat16)
                mixed = jnp.dot(grad, right_tiles[slot], preferred_element_type=jnp.float32)
                left_part = left_part + (
                    mixed.reshape(tile // 8, 8, width) * w_wide[k][None]
                ).reshape(tile, width)
                bin_out[k] += (mixed * left_wide).reshape(tile // 8, 8, width).sum(0)
                pieces.append(grad)
                scales.append(left_turn[...] * w_cols[k])
            left_sum[...] += left_part
            right_sum[...] += jnp.dot(
                jnp.concatenate(scales, 1),
                jnp.concatenate(pieces, 0),
                preferred_element_type=jnp.float32,
            )
            return 0

        lax.fori_loop(0, bins // GROUP_GRADS, grads, 0)
        left_grads[slot] = left_sum[...].astype(jnp.bfloat16)
        right_grads[slot] = right_sum[...].T.astype(jnp.bfloat16)
        return 0

    lax.fori_loop(0, live, block, 0)


def run_blocks(place, count, bin_weight, bin_bias, left_from, right_from, teacher):
    slots, bins, tile, _ = teacher.shape
    width = bin_weight.shape[0]
    wide = bin_weight.astype(jnp.float32)
    smem = pl.BlockSpec(memory_space=pltpu.SMEM)
    vmem = pl.BlockSpec(memory_space=pltpu.VMEM)
    hbm = pl.BlockSpec(memory_space=pl.ANY)
    f32, bf16 = jnp.float32, jnp.bfloat16
    piece = jax.ShapeDtypeStruct((slots, tile, width), bf16)
    return pl.pallas_call(
        blocks_kernel,
        out_shape=[piece] * 2
        + [
            jax.ShapeDtypeStruct((bins, 8, width), f32),
            jax.ShapeDtypeStruct((8, tile), f32),
        ],
        in_specs=[smem] * 3 + [vmem] * 2 + [hbm] * 9,
        out_specs=[vmem] * 4,
        scratch_shapes=[
            pltpu.VMEM((bins, 16, width), bf16),
            pltpu.VMEM((bins, 8, width), f32),
            pltpu.VMEM((bins, width, tile), bf16),
            pltpu.VMEM((slots, tile, width), bf16),
            pltpu.VMEM((slots, tile, width), bf16),
            pltpu.VMEM((2, bins, tile, tile), bf16),
            pltpu.VMEM((bins, tile, tile), f32),
            pltpu.VMEM((width, tile), bf16),
            pltpu.VMEM((width, tile), bf16),
            pltpu.VMEM((tile, width), f32),
            pltpu.VMEM((width, tile), f32),
            pltpu.SemaphoreType.DMA((slots, 2)),
            pltpu.SemaphoreType.DMA((2,)),
        ],
        compiler_params=pltpu.CompilerParams(vmem_limit_bytes=48 * 1024 * 1024),
        cost_estimate=pl.CostEstimate(
            flops=6 * 8 * 64 * 128**3, bytes_accessed=20 * 2**20, transcendentals=8 * 2**20
        ),
    )(place, count, bin_bias, wide.T, wide, *left_from, *right_from, teacher)


AXES = ("z", "core", "y", "x")
TILES_DEV = 4


def own_spot(info, s, slot):
    row = info[s, 2 * slot]
    return lax.rem(row // 16, 4), lax.rem(row // 4, 4), lax.rem(row, 4)


def pick_kernel(info, here, near0, near1, near2, near3, out0, out1, out2, out3, bank):
    outs = (out0, out1, out2, out3)
    for n, near in enumerate((near0, near1, near2, near3)):
        bank[pl.ds(4 * n, 4)] = near[...]
    slots = out0.shape[0]
    for s in range(4):
        for slot in range(slots):
            _, x, t = own_spot(info, s, slot)
            spot = lax.rem(here[3] - x + 4, 4) * 4 + t
            outs[(4 - s) % 4][slot] = bank[spot]


def pick_tiles(info, here, near):
    slots = (info.shape[1] - 1) // 2
    _, tile, width = near[0].shape
    smem = pl.BlockSpec(memory_space=pltpu.SMEM)
    vmem = pl.BlockSpec(memory_space=pltpu.VMEM)
    return pl.pallas_call(
        pick_kernel,
        out_shape=[jax.ShapeDtypeStruct((slots, tile, width), near[0].dtype)] * 4,
        in_specs=[smem] * 2 + [vmem] * 4,
        out_specs=[vmem] * 4,
        scratch_shapes=[pltpu.VMEM((16, tile, width), near[0].dtype)],
        compiler_params=pltpu.CompilerParams(vmem_limit_bytes=16 * 1024 * 1024),
    )(info, here, *near)


def fold_kernel(side, info, here, *refs):
    sources, (own, far1, far2, far3, total) = refs[:-5], refs[-5:]
    total[...] = jnp.zeros(total.shape, jnp.float32)
    slots = sources[0].shape[0]
    for s, source in enumerate(sources):
        live = info[s, 2 * slots if side == 0 else 3 * slots]
        for slot in range(slots):
            if side == 0:
                y, x, t = own_spot(info, s, slot)
                mine, spot = y == here[2], lax.rem(x - here[3] + 4, 4) * 4 + t
            else:
                z, core, u = (info[s, n * slots + slot] for n in range(3))
                mine, spot = core == here[1], lax.rem(z - here[0] + 4, 4) * 4 + u

            @pl.when((slot < live) & mine)
            def _():
                total[spot] += source[slot].astype(jnp.float32)

    own[...] = total[pl.ds(0, 4)]
    for n, far in enumerate((far1, far2, far3)):
        far[...] = total[pl.ds(4 * n + 4, 4)].astype(jnp.bfloat16)


def fold_slots(side, info, here, sources):
    _, tile, width = sources[0].shape
    smem = pl.BlockSpec(memory_space=pltpu.SMEM)
    vmem = pl.BlockSpec(memory_space=pltpu.VMEM)
    far = jax.ShapeDtypeStruct((4, tile, width), jnp.bfloat16)
    return pl.pallas_call(
        functools.partial(fold_kernel, side),
        out_shape=[jax.ShapeDtypeStruct((4, tile, width), jnp.float32)] + [far] * 3,
        in_specs=[smem] * 2 + [vmem] * len(sources),
        out_specs=[vmem] * 4,
        scratch_shapes=[pltpu.VMEM((16, tile, width), jnp.float32)],
        compiler_params=pltpu.CompilerParams(vmem_limit_bytes=16 * 1024 * 1024),
    )(info, here, *sources)


def shift(value, axis, step):
    size = lax.axis_size(axis)
    return lax.ppermute(value, axis, [(i, (i + step) % size) for i in range(size)])


def ring(value, axis):
    return [shift(value, axis, s) for s in range(1, lax.axis_size(axis))]


def after(value, *others):
    return lax.optimization_barrier((value,) + others)[0]


def low_parts(value, count):
    parts = []
    for _ in range(count):
        parts.append(value.astype(jnp.bfloat16))
        value = value - parts[-1].astype(jnp.float32)
    return parts


def per_device(
    single, left_weight, right_weight, bin_weight, bin_bias, block_tiles, block_count, teacher
):
    slots, bins, tile = teacher.shape[1:4]
    devices = lax.axis_size(AXES)
    own_tiles = block_tiles[0]
    left_wide = left_weight.astype(jnp.float32)
    right_wide = right_weight.astype(jnp.float32)
    info = jnp.concatenate([own_tiles.reshape(1, -1), block_count[None]], axis=1)
    left_local = jnp.dot(single, left_weight, preferred_element_type=jnp.float32).astype(
        jnp.bfloat16
    )
    rows_dev, width = left_local.shape
    left_local = left_local.reshape(-1, tile, width)
    here = jnp.stack([lax.axis_index(a) for a in AXES]).astype(jnp.int32)
    z, core, y = here[0], here[1], here[2]
    left_near = [left_local] + ring(left_local, "x")
    info_first = after(info, left_local)
    right_local = jnp.dot(after(single, left_near[1]), right_weight, preferred_element_type=jnp.float32).astype(
        jnp.bfloat16
    )
    right_local = right_local.reshape(-1, tile, width)
    info_y = jnp.concatenate([info_first] + ring(info_first, "y"))
    picked = pick_tiles(info_y, here, left_near)
    left_from = [picked[0]] + [shift(picked[s], "y", s) for s in (1, 2, 3)]
    row, col = own_tiles[:, 0], own_tiles[:, 1]
    lists = jnp.concatenate([col // 128 % 4, col // 64 % 2, col % TILES_DEV, block_count])[None]
    packed = jnp.pad(lists.astype(jnp.bfloat16), ((0, 15), (0, width - lists.shape[1])))
    sibling = shift(jnp.concatenate([right_local.reshape(rows_dev, width), packed]), "core", 1)
    far_lists = sibling[rows_dev : rows_dev + 1, : lists.shape[1]].astype(jnp.int32)
    info_core = jnp.concatenate([lists, far_lists])
    right_pair = jnp.concatenate([right_local, sibling[:rows_dev].reshape(-1, tile, width)])
    right_pair = after(right_pair, *picked)
    right_from = [right_pair] + ring(right_pair, "z")
    place = jnp.stack(
        [
            (y - row // 16 % 4) % 4,
            (z - col // 128 % 4) % 4,
            (core - col // 64 % 2) % 2 * TILES_DEV + col % TILES_DEV,
        ],
        axis=1,
    )
    place = after(place, info_core)
    left_slots, right_slots, bins_part, cross_part = run_blocks(
        place, block_count, bin_weight, bin_bias, left_from, right_from, teacher[0]
    )
    left_ring = ring(left_slots, "y")
    right_ring = ring(right_slots, "core")
    right_rows_grad, *right_far = fold_slots(1, info_core, here, [right_slots] + right_ring)
    right_far = [shift(right_far[s - 1], "z", s) for s in (1, 2, 3)]
    left_ring = after(left_ring, *right_far)
    left_rows_grad, *left_far = fold_slots(0, info_y, here, [left_slots] + left_ring)
    for s in (1, 2, 3):
        left_rows_grad = left_rows_grad + shift(left_far[s - 1], "x", s).astype(jnp.float32)
        right_rows_grad = right_rows_grad + right_far[s - 1].astype(jnp.float32)
    left_rows_grad = left_rows_grad.reshape(rows_dev, width)
    right_rows_grad = right_rows_grad.reshape(rows_dev, width)
    single_wide = single.astype(jnp.float32)
    part_left = jnp.dot(single_wide.T, left_rows_grad, precision=lax.Precision.HIGHEST)
    part_right = jnp.dot(single_wide.T, right_rows_grad, precision=lax.Precision.HIGHEST)
    depth = part_left.shape[0]
    rows_sum = 2 * depth + bins
    chunk = rows_sum // devices + 1
    last = rows_sum // chunk, rows_sum % chunk
    bf16, f32 = jnp.bfloat16, jnp.float32
    scalars = jnp.stack(low_parts(jnp.sum(cross_part), 3) + [block_count[0].astype(bf16)])
    packed = jnp.concatenate(
        [
            part_left.astype(bf16),
            part_right.astype(bf16),
            jnp.sum(bins_part, axis=1).astype(bf16),
            jnp.pad(scalars[None], ((0, chunk * devices - rows_sum - 1), (0, width - 4))),
        ]
    ).reshape(devices, chunk, width)
    mine = jnp.sum(lax.all_to_all(packed, AXES, 0, 0).astype(f32), axis=0)
    high, low = low_parts(mine, 2)
    mine = jnp.concatenate([high, low[last[1] : last[1] + 1]])
    totals = lax.all_to_all(
        jnp.broadcast_to(mine[None], (devices, chunk + 1, width)), AXES, 0, 0
    ).astype(f32)
    scalars = totals[last[0], last[1]] + totals[last[0], chunk]
    totals = totals[:, :chunk].reshape(-1, width)
    grad_single = (
        jnp.dot(left_rows_grad, left_wide.T, precision=lax.Precision.HIGHEST)
        + jnp.dot(right_rows_grad, right_wide.T, precision=lax.Precision.HIGHEST)
    ).astype(jnp.bfloat16)
    grad_left = totals[:depth] / devices
    grad_right = totals[depth : 2 * depth] / devices
    grad_bin = totals[2 * depth : rows_sum].T / devices
    cross_total = scalars[0] + scalars[1] + scalars[2]
    loss_value = cross_total / (scalars[3] * (tile * tile))
    return (grad_single, grad_left, grad_right, grad_bin, loss_value)


def solution(mesh):
    torus = Mesh(mesh.devices.reshape(4, 2, 4, 4), AXES)
    return jax.shard_map(
        per_device,
        mesh=torus,
        in_specs=(
            P(AXES, None),
            P(),
            P(),
            P(),
            P(),
            P(AXES, None, None),
            P(AXES),
            P(AXES, None, None, None, None),
        ),
        out_specs=(P(AXES, None), P(), P(), P(), P()),
        check_vma=False,
    )
```

```python
import functools
import jax
import jax.numpy as jnp
from jax import lax
from jax.experimental import pallas as pl
from jax.experimental.pallas import tpu as pltpu
from jax.sharding import Mesh
from jax.sharding import PartitionSpec as P

GROUP_SCORES = 32
GROUP_SOFT = 16
GROUP_GRADS = 32


def blocks_kernel(
    place, count, bias, w_turned, w_plain, left0, left1, left2, left3, right0, right1, teacher,
    left_grads, right_grads, bin_out, cross_out,
    w_rows, w_wide, w_cols, left_tiles, right_tiles, target, logit, left_turn, right_turn, left_sum, right_sum,
    tile_sem, target_sem,
):
    left_from = (left0, left1, left2, left3)
    right_from = (right0, right1)
    slots, bins, tile, width = teacher.shape
    live = count[0]

    def target_copy(slot):
        return pltpu.make_async_copy(
            teacher.at[slot], target.at[lax.rem(slot, 2)], target_sem.at[lax.rem(slot, 2)]
        )

    def left_copy(slot, n):
        return pltpu.make_async_copy(
            left_from[n].at[slot], left_tiles.at[slot], tile_sem.at[slot, 0]
        )

    def right_copy(slot, n):
        return pltpu.make_async_copy(
            right_from[n].at[pl.ds(pl.multiple_of(place[slot, 2] * tile, tile), tile)],
            right_tiles.at[slot], tile_sem.at[slot, 1]
        )

    for slot in range(slots):
        for n in range(len(left_from)):

            @pl.when((slot < live) & (place[slot, 0] == n))
            def _():
                left_copy(slot, n).start()

        for n in range(len(right_from)):

            @pl.when((slot < live) & (place[slot, 1] == n))
            def _():
                right_copy(slot, n).start()

    target_copy(0).start()
    for k in range(bins):
        row = w_turned[k : k + 1, :]
        w_wide[k] = jnp.broadcast_to(row, (8, width))
        w_rows[k] = jnp.broadcast_to(row, (16, width)).astype(jnp.bfloat16)
        w_cols[k] = jnp.broadcast_to(w_plain[:, k : k + 1], (width, tile)).astype(jnp.bfloat16)
    bin_out[...] = jnp.zeros(bin_out.shape, jnp.float32)
    cross_out[...] = jnp.zeros(cross_out.shape, jnp.float32)

    def block(slot, _):
        buf = lax.rem(slot, 2)

        @pl.when(slot + 1 < live)
        def _():
            target_copy(slot + 1).start()

        left_copy(slot, 0).wait()
        right_copy(slot, 0).wait()
        left = left_tiles[slot]
        right = right_tiles[slot]
        left_turn[...] = left.T
        right_turn[...] = right.T
        left_sum[...] = jnp.zeros(left_sum.shape, jnp.float32)
        right_sum[...] = jnp.zeros(right_sum.shape, jnp.float32)

        def scores(g, highest):
            left = left_tiles[slot].reshape(tile // 16, 16, width)
            for j in range(GROUP_SCORES):
                k = g * GROUP_SCORES + j
                scaled = (left * w_rows[k][None]).reshape(tile, width)
                value = jnp.dot(scaled, right_turn[...], preferred_element_type=jnp.float32)
                value = value + bias[k]
                logit[k] = value
                highest = jnp.maximum(highest, value)
            return highest

        highest = lax.fori_loop(
            0, bins // GROUP_SCORES, scores, jnp.full((tile, tile), -jnp.inf, jnp.float32)
        )
        target_copy(slot).wait()

        STEP = 32
        ratios = []
        for p in range(0, tile, STEP):
            rows = pl.ds(p, STEP)
            top = highest[p : p + STEP]

            def soft(g, carried):
                total, mass, cross = carried
                for j in range(GROUP_SOFT):
                    k = g * GROUP_SOFT + j
                    value = logit[k, rows, :] - top
                    power = jnp.exp(value)
                    goal = target[buf, k, rows, :].astype(jnp.float32)
                    total = total + power
                    mass = mass + goal
                    cross = cross + goal * value
                    logit[k, rows, :] = power
                return total, mass, cross

            zero = jnp.zeros((STEP, tile), jnp.float32)
            total, mass, cross = lax.fori_loop(0, bins // GROUP_SOFT, soft, (zero, zero, zero))
            cross = mass * jnp.log(total) - cross
            cross_out[...] += cross.reshape(STEP // 8, 8, tile).sum(0)
            ratios.append(mass / total)
        ratio = jnp.concatenate(ratios, 0)

        def grads(g, _):
            left_wide = left_tiles[slot].astype(jnp.float32)
            pieces, scales = [], []
            left_part = jnp.zeros((tile, width), jnp.float32)
            for j in range(GROUP_GRADS):
                k = g * GROUP_GRADS + j
                grad = logit[k] * ratio - target[buf, k].astype(jnp.float32)
                grad = grad.astype(jnp.bfloat16)
                mixed = jnp.dot(grad, right_tiles[slot], preferred_element_type=jnp.float32)
                left_part = left_part + (
                    mixed.reshape(tile // 8, 8, width) * w_wide[k][None]
                ).reshape(tile, width)
                bin_out[k] += (mixed * left_wide).reshape(tile // 8, 8, width).sum(0)
                pieces.append(grad)
                scales.append(left_turn[...] * w_cols[k])
            left_sum[...] += left_part
            right_sum[...] += jnp.dot(
                jnp.concatenate(scales, 1),
                jnp.concatenate(pieces, 0),
                preferred_element_type=jnp.float32,
            )
            return 0

        lax.fori_loop(0, bins // GROUP_GRADS, grads, 0)
        left_grads[slot] = left_sum[...].astype(jnp.bfloat16)
        right_grads[slot] = right_sum[...].T.astype(jnp.bfloat16)
        return 0

    lax.fori_loop(0, live, block, 0)


def run_blocks(place, count, bin_weight, bin_bias, left_from, right_from, teacher):
    slots, bins, tile, _ = teacher.shape
    width = bin_weight.shape[0]
    wide = bin_weight.astype(jnp.float32)
    smem = pl.BlockSpec(memory_space=pltpu.SMEM)
    vmem = pl.BlockSpec(memory_space=pltpu.VMEM)
    hbm = pl.BlockSpec(memory_space=pl.ANY)
    f32, bf16 = jnp.float32, jnp.bfloat16
    piece = jax.ShapeDtypeStruct((slots, tile, width), bf16)
    return pl.pallas_call(
        blocks_kernel,
        out_shape=[piece] * 2
        + [
            jax.ShapeDtypeStruct((bins, 8, width), f32),
            jax.ShapeDtypeStruct((8, tile), f32),
        ],
        in_specs=[smem] * 3 + [vmem] * 2 + [hbm] * 7,
        out_specs=[vmem] * 4,
        scratch_shapes=[
            pltpu.VMEM((bins, 16, width), bf16),
            pltpu.VMEM((bins, 8, width), f32),
            pltpu.VMEM((bins, width, tile), bf16),
            pltpu.VMEM((slots, tile, width), bf16),
            pltpu.VMEM((slots, tile, width), bf16),
            pltpu.VMEM((2, bins, tile, tile), bf16),
            pltpu.VMEM((bins, tile, tile), f32),
            pltpu.VMEM((width, tile), bf16),
            pltpu.VMEM((width, tile), bf16),
            pltpu.VMEM((tile, width), f32),
            pltpu.VMEM((width, tile), f32),
            pltpu.SemaphoreType.DMA((slots, 2)),
            pltpu.SemaphoreType.DMA((2,)),
        ],
        compiler_params=pltpu.CompilerParams(vmem_limit_bytes=48 * 1024 * 1024),
        cost_estimate=pl.CostEstimate(
            flops=6 * 8 * 64 * 128**3, bytes_accessed=20 * 2**20, transcendentals=8 * 2**20
        ),
    )(place, count, bin_bias, wide.T, wide, *left_from, *right_from, teacher)


AXES = ("z", "core", "y", "x")
TILES_DEV = 4


def own_spot(info, s, slot):
    row = info[s, 2 * slot]
    return lax.rem(row // 16, 4), lax.rem(row // 4, 4), lax.rem(row, 4)


def pick_kernel(info, here, near0, near1, near2, near3, out0, out1, out2, out3, bank):
    outs = (out0, out1, out2, out3)
    for n, near in enumerate((near0, near1, near2, near3)):
        bank[pl.ds(4 * n, 4)] = near[...]
    slots = out0.shape[0]
    for s in range(4):
        for slot in range(slots):
            _, x, t = own_spot(info, s, slot)
            spot = lax.rem(here[3] - x + 4, 4) * 4 + t
            outs[(4 - s) % 4][slot] = bank[spot]


def pick_tiles(info, here, near):
    slots = (info.shape[1] - 1) // 2
    _, tile, width = near[0].shape
    smem = pl.BlockSpec(memory_space=pltpu.SMEM)
    vmem = pl.BlockSpec(memory_space=pltpu.VMEM)
    return pl.pallas_call(
        pick_kernel,
        out_shape=[jax.ShapeDtypeStruct((slots, tile, width), near[0].dtype)] * 4,
        in_specs=[smem] * 2 + [vmem] * 4,
        out_specs=[vmem] * 4,
        scratch_shapes=[pltpu.VMEM((16, tile, width), near[0].dtype)],
        compiler_params=pltpu.CompilerParams(vmem_limit_bytes=16 * 1024 * 1024),
    )(info, here, *near)


def fold_kernel(side, info, here, *refs):
    sources, (own, far1, far2, far3, total) = refs[:-5], refs[-5:]
    total[...] = jnp.zeros(total.shape, jnp.float32)
    slots = sources[0].shape[0]
    for s, source in enumerate(sources):
        live = info[s, 2 * slots if side == 0 else 3 * slots]
        for slot in range(slots):
            if side == 0:
                y, x, t = own_spot(info, s, slot)
                mine, spot = y == here[2], lax.rem(x - here[3] + 4, 4) * 4 + t
            else:
                z, core, u = (info[s, n * slots + slot] for n in range(3))
                mine, spot = core == here[1], lax.rem(z - here[0] + 4, 4) * 4 + u

            @pl.when((slot < live) & mine)
            def _():
                total[spot] += source[slot].astype(jnp.float32)

    own[...] = total[pl.ds(0, 4)]
    for n, far in enumerate((far1, far2, far3)):
        far[...] = total[pl.ds(4 * n + 4, 4)].astype(jnp.bfloat16)


def fold_slots(side, info, here, sources):
    _, tile, width = sources[0].shape
    smem = pl.BlockSpec(memory_space=pltpu.SMEM)
    vmem = pl.BlockSpec(memory_space=pltpu.VMEM)
    far = jax.ShapeDtypeStruct((4, tile, width), jnp.bfloat16)
    return pl.pallas_call(
        functools.partial(fold_kernel, side),
        out_shape=[jax.ShapeDtypeStruct((4, tile, width), jnp.float32)] + [far] * 3,
        in_specs=[smem] * 2 + [vmem] * len(sources),
        out_specs=[vmem] * 4,
        scratch_shapes=[pltpu.VMEM((16, tile, width), jnp.float32)],
        compiler_params=pltpu.CompilerParams(vmem_limit_bytes=16 * 1024 * 1024),
    )(info, here, *sources)


def shift(value, axis, step):
    size = lax.axis_size(axis)
    return lax.ppermute(value, axis, [(i, (i + step) % size) for i in range(size)])


def ring(value, axis):
    return [shift(value, axis, s) for s in range(1, lax.axis_size(axis))]


def after(value, *others):
    return lax.optimization_barrier((value,) + others)[0]


def low_parts(value, count):
    parts = []
    for _ in range(count):
        parts.append(value.astype(jnp.bfloat16))
        value = value - parts[-1].astype(jnp.float32)
    return parts


def per_device(
    single, left_weight, right_weight, bin_weight, bin_bias, block_tiles, block_count, teacher
):
    slots, bins, tile = teacher.shape[1:4]
    devices = lax.axis_size(AXES)
    own_tiles = block_tiles[0]
    left_wide = left_weight.astype(jnp.float32)
    right_wide = right_weight.astype(jnp.float32)
    info = jnp.concatenate([own_tiles.reshape(1, -1), block_count[None]], axis=1)
    left_local = jnp.dot(single, left_weight, preferred_element_type=jnp.float32).astype(
        jnp.bfloat16
    )
    rows_dev, width = left_local.shape
    left_local = left_local.reshape(-1, tile, width)
    here = jnp.stack([lax.axis_index(a) for a in AXES]).astype(jnp.int32)
    z, core, y = here[0], here[1], here[2]
    left_near = [left_local] + ring(left_local, "x")
    right_local = jnp.dot(after(single, left_near[1]), right_weight, preferred_element_type=jnp.float32).astype(
        jnp.bfloat16
    )
    right_local = right_local.reshape(-1, tile, width)
    right_ring = ring(right_local, "z")
    info_first = after(info, left_local)
    info_y = jnp.concatenate([info_first] + ring(info_first, "y"))
    picked = pick_tiles(info_y, here, left_near)
    left_from = [picked[0]] + [shift(picked[s], "y", s) for s in (1, 2, 3)]
    row, col = own_tiles[:, 0], own_tiles[:, 1]
    right_ring = after(right_ring, *left_from)
    lists = jnp.concatenate([col // 128 % 4, col // 64 % 2, col % TILES_DEV, block_count])[None]
    packed = jnp.pad(lists.astype(jnp.bfloat16), ((0, 15), (0, width - lists.shape[1])))
    right_near = jnp.concatenate(
        [part.reshape(rows_dev, width) for part in [right_local] + right_ring] + [packed]
    )
    sibling = shift(right_near, "core", 1)
    far_lists = sibling[-16:-15, : lists.shape[1]].astype(jnp.int32)
    info_core = jnp.concatenate([lists, far_lists])
    right_from = [right_near, sibling]
    place = jnp.stack(
        [
            (y - row // 16 % 4) % 4,
            (core - col // 64 % 2) % 2,
            (z - col // 128 % 4) % 4 * TILES_DEV + col % TILES_DEV,
        ],
        axis=1,
    )
    place = after(place, info_core)
    left_slots, right_slots, bins_part, cross_part = run_blocks(
        place, block_count, bin_weight, bin_bias, left_from, right_from, teacher[0]
    )
    left_ring = ring(left_slots, "y")
    right_ring = ring(right_slots, "core")
    right_rows_grad, *right_far = fold_slots(1, info_core, here, [right_slots] + right_ring)
    right_far = [shift(right_far[s - 1], "z", s) for s in (1, 2, 3)]
    left_ring = after(left_ring, *right_far)
    left_rows_grad, *left_far = fold_slots(0, info_y, here, [left_slots] + left_ring)
    for s in (1, 2, 3):
        left_rows_grad = left_rows_grad + shift(left_far[s - 1], "x", s).astype(jnp.float32)
        right_rows_grad = right_rows_grad + right_far[s - 1].astype(jnp.float32)
    left_rows_grad = left_rows_grad.reshape(rows_dev, width)
    right_rows_grad = right_rows_grad.reshape(rows_dev, width)
    single_wide = single.astype(jnp.float32)
    part_left = jnp.dot(single_wide.T, left_rows_grad, precision=lax.Precision.HIGHEST)
    part_right = jnp.dot(single_wide.T, right_rows_grad, precision=lax.Precision.HIGHEST)
    depth = part_left.shape[0]
    rows_sum = 2 * depth + bins
    chunk = rows_sum // devices + 1
    last = rows_sum // chunk, rows_sum % chunk
    bf16, f32 = jnp.bfloat16, jnp.float32
    scalars = jnp.stack(low_parts(jnp.sum(cross_part), 3) + [block_count[0].astype(bf16)])
    packed = jnp.concatenate(
        [
            part_left.astype(bf16),
            part_right.astype(bf16),
            jnp.sum(bins_part, axis=1).astype(bf16),
            jnp.pad(scalars[None], ((0, chunk * devices - rows_sum - 1), (0, width - 4))),
        ]
    ).reshape(devices, chunk, width)
    mine = jnp.sum(lax.all_to_all(packed, AXES, 0, 0).astype(f32), axis=0)
    high, low = low_parts(mine, 2)
    mine = jnp.concatenate([high, low[last[1] : last[1] + 1]])
    totals = lax.all_to_all(
        jnp.broadcast_to(mine[None], (devices, chunk + 1, width)), AXES, 0, 0
    ).astype(f32)
    scalars = totals[last[0], last[1]] + totals[last[0], chunk]
    totals = totals[:, :chunk].reshape(-1, width)
    grad_single = (
        jnp.dot(left_rows_grad, left_wide.T, precision=lax.Precision.HIGHEST)
        + jnp.dot(right_rows_grad, right_wide.T, precision=lax.Precision.HIGHEST)
    ).astype(jnp.bfloat16)
    grad_left = totals[:depth] / devices
    grad_right = totals[depth : 2 * depth] / devices
    grad_bin = totals[2 * depth : rows_sum].T / devices
    cross_total = scalars[0] + scalars[1] + scalars[2]
    loss_value = cross_total / (scalars[3] * (tile * tile))
    return (grad_single, grad_left, grad_right, grad_bin, loss_value)


def solution(mesh):
    torus = Mesh(mesh.devices.reshape(4, 2, 4, 4), AXES)
    return jax.shard_map(
        per_device,
        mesh=torus,
        in_specs=(
            P(AXES, None),
            P(),
            P(),
            P(),
            P(),
            P(AXES, None, None),
            P(AXES),
            P(AXES, None, None, None, None),
        ),
        out_specs=(P(AXES, None), P(), P(), P(), P()),
        check_vma=False,
    )
```

```python
import functools
import jax
import jax.numpy as jnp
from jax import lax
from jax.experimental import pallas as pl
from jax.experimental.pallas import tpu as pltpu
from jax.sharding import Mesh
from jax.sharding import PartitionSpec as P

GROUP_SCORES = 64
GROUP_SOFT = 16
GROUP_GRADS = 64


def blocks_kernel(
    place, count, bias, w_turned, w_plain, left0, left1, left2, left3, right0, right1, teacher,
    left_grads, right_grads, bin_out, cross_out,
    w_rows, w_wide, w_cols, left_tiles, right_tiles, target, logit, left_turn, right_turn, left_sum, right_sum,
    tile_sem, target_sem,
):
    left_from = (left0, left1, left2, left3)
    right_from = (right0, right1)
    slots, bins, tile, width = teacher.shape
    live = count[0]

    def target_copy(slot):
        return pltpu.make_async_copy(
            teacher.at[slot], target.at[lax.rem(slot, 2)], target_sem.at[lax.rem(slot, 2)]
        )

    def left_copy(slot, n):
        return pltpu.make_async_copy(
            left_from[n].at[slot], left_tiles.at[slot], tile_sem.at[slot, 0]
        )

    def right_copy(slot, n):
        return pltpu.make_async_copy(
            right_from[n].at[pl.ds(pl.multiple_of(place[slot, 2] * tile, tile), tile)],
            right_tiles.at[slot], tile_sem.at[slot, 1]
        )

    for slot in range(slots):
        for n in range(len(left_from)):

            @pl.when((slot < live) & (place[slot, 0] == n))
            def _():
                left_copy(slot, n).start()

        for n in range(len(right_from)):

            @pl.when((slot < live) & (place[slot, 1] == n))
            def _():
                right_copy(slot, n).start()

    target_copy(0).start()
    for k in range(bins):
        row = w_turned[k : k + 1, :]
        w_wide[k] = jnp.broadcast_to(row, (8, width))
        w_rows[k] = jnp.broadcast_to(row, (16, width)).astype(jnp.bfloat16)
        w_cols[k] = jnp.broadcast_to(w_plain[:, k : k + 1], (width, tile)).astype(jnp.bfloat16)
    bin_out[...] = jnp.zeros(bin_out.shape, jnp.float32)
    cross_out[...] = jnp.zeros(cross_out.shape, jnp.float32)

    def block(slot, _):
        buf = lax.rem(slot, 2)

        @pl.when(slot + 1 < live)
        def _():
            target_copy(slot + 1).start()

        left_copy(slot, 0).wait()
        right_copy(slot, 0).wait()
        left = left_tiles[slot]
        right = right_tiles[slot]
        left_turn[...] = left.T
        right_turn[...] = right.T
        left_sum[...] = jnp.zeros(left_sum.shape, jnp.float32)
        right_sum[...] = jnp.zeros(right_sum.shape, jnp.float32)

        def scores(g, highest):
            left = left_tiles[slot].reshape(tile // 16, 16, width)
            for j in range(GROUP_SCORES):
                k = g * GROUP_SCORES + j
                scaled = (left * w_rows[k][None]).reshape(tile, width)
                value = jnp.dot(scaled, right_turn[...], preferred_element_type=jnp.float32)
                value = value + bias[k]
                logit[k] = value
                highest = jnp.maximum(highest, value)
            return highest

        highest = lax.fori_loop(
            0, bins // GROUP_SCORES, scores, jnp.full((tile, tile), -jnp.inf, jnp.float32)
        )
        target_copy(slot).wait()

        STEP = 32
        ratios = []
        for p in range(0, tile, STEP):
            rows = pl.ds(p, STEP)
            top = highest[p : p + STEP]

            def soft(g, carried):
                total, mass, cross = carried
                for j in range(GROUP_SOFT):
                    k = g * GROUP_SOFT + j
                    value = logit[k, rows, :] - top
                    power = jnp.exp(value)
                    goal = target[buf, k, rows, :].astype(jnp.float32)
                    total = total + power
                    mass = mass + goal
                    cross = cross + goal * value
                    logit[k, rows, :] = power
                return total, mass, cross

            zero = jnp.zeros((STEP, tile), jnp.float32)
            total, mass, cross = lax.fori_loop(0, bins // GROUP_SOFT, soft, (zero, zero, zero))
            cross = mass * jnp.log(total) - cross
            cross_out[...] += cross.reshape(STEP // 8, 8, tile).sum(0)
            ratios.append(mass / total)
        ratio = jnp.concatenate(ratios, 0)

        def grads(g, _):
            left_wide = left_tiles[slot].astype(jnp.float32)
            pieces, scales = [], []
            left_part = jnp.zeros((tile, width), jnp.float32)
            for j in range(GROUP_GRADS):
                k = g * GROUP_GRADS + j
                grad = logit[k] * ratio - target[buf, k].astype(jnp.float32)
                grad = grad.astype(jnp.bfloat16)
                mixed = jnp.dot(grad, right_tiles[slot], preferred_element_type=jnp.float32)
                left_part = left_part + (
                    mixed.reshape(tile // 8, 8, width) * w_wide[k][None]
                ).reshape(tile, width)
                bin_out[k] += (mixed * left_wide).reshape(tile // 8, 8, width).sum(0)
                pieces.append(grad)
                scales.append(left_turn[...] * w_cols[k])
            left_sum[...] += left_part
            right_sum[...] += jnp.dot(
                jnp.concatenate(scales, 1),
                jnp.concatenate(pieces, 0),
                preferred_element_type=jnp.float32,
            )
            return 0

        lax.fori_loop(0, bins // GROUP_GRADS, grads, 0)
        left_grads[slot] = left_sum[...].astype(jnp.bfloat16)
        right_grads[slot] = right_sum[...].T.astype(jnp.bfloat16)
        return 0

    lax.fori_loop(0, live, block, 0)


def run_blocks(place, count, bin_weight, bin_bias, left_from, right_from, teacher):
    slots, bins, tile, _ = teacher.shape
    width = bin_weight.shape[0]
    wide = bin_weight.astype(jnp.float32)
    smem = pl.BlockSpec(memory_space=pltpu.SMEM)
    vmem = pl.BlockSpec(memory_space=pltpu.VMEM)
    hbm = pl.BlockSpec(memory_space=pl.ANY)
    f32, bf16 = jnp.float32, jnp.bfloat16
    piece = jax.ShapeDtypeStruct((slots, tile, width), bf16)
    return pl.pallas_call(
        blocks_kernel,
        out_shape=[piece] * 2
        + [
            jax.ShapeDtypeStruct((bins, 8, width), f32),
            jax.ShapeDtypeStruct((8, tile), f32),
        ],
        in_specs=[smem] * 3 + [vmem] * 2 + [hbm] * 7,
        out_specs=[vmem] * 4,
        scratch_shapes=[
            pltpu.VMEM((bins, 16, width), bf16),
            pltpu.VMEM((bins, 8, width), f32),
            pltpu.VMEM((bins, width, tile), bf16),
            pltpu.VMEM((slots, tile, width), bf16),
            pltpu.VMEM((slots, tile, width), bf16),
            pltpu.VMEM((2, bins, tile, tile), bf16),
            pltpu.VMEM((bins, tile, tile), f32),
            pltpu.VMEM((width, tile), bf16),
            pltpu.VMEM((width, tile), bf16),
            pltpu.VMEM((tile, width), f32),
            pltpu.VMEM((width, tile), f32),
            pltpu.SemaphoreType.DMA((slots, 2)),
            pltpu.SemaphoreType.DMA((2,)),
        ],
        compiler_params=pltpu.CompilerParams(vmem_limit_bytes=48 * 1024 * 1024),
        cost_estimate=pl.CostEstimate(
            flops=6 * 8 * 64 * 128**3, bytes_accessed=20 * 2**20, transcendentals=8 * 2**20
        ),
    )(place, count, bin_bias, wide.T, wide, *left_from, *right_from, teacher)


AXES = ("z", "core", "y", "x")
TILES_DEV = 4


def own_spot(info, s, slot):
    row = info[s, 2 * slot]
    return lax.rem(row // 16, 4), lax.rem(row // 4, 4), lax.rem(row, 4)


def pick_kernel(info, here, near0, near1, near2, near3, out0, out1, out2, out3, bank):
    outs = (out0, out1, out2, out3)
    for n, near in enumerate((near0, near1, near2, near3)):
        bank[pl.ds(4 * n, 4)] = near[...]
    slots = out0.shape[0]
    for s in range(4):
        for slot in range(slots):
            _, x, t = own_spot(info, s, slot)
            spot = lax.rem(here[3] - x + 4, 4) * 4 + t
            outs[(4 - s) % 4][slot] = bank[spot]


def pick_tiles(info, here, near):
    slots = (info.shape[1] - 1) // 2
    _, tile, width = near[0].shape
    smem = pl.BlockSpec(memory_space=pltpu.SMEM)
    vmem = pl.BlockSpec(memory_space=pltpu.VMEM)
    return pl.pallas_call(
        pick_kernel,
        out_shape=[jax.ShapeDtypeStruct((slots, tile, width), near[0].dtype)] * 4,
        in_specs=[smem] * 2 + [vmem] * 4,
        out_specs=[vmem] * 4,
        scratch_shapes=[pltpu.VMEM((16, tile, width), near[0].dtype)],
        compiler_params=pltpu.CompilerParams(vmem_limit_bytes=16 * 1024 * 1024),
    )(info, here, *near)


def fold_kernel(side, info, here, *refs):
    sources, (own, far1, far2, far3, total) = refs[:-5], refs[-5:]
    total[...] = jnp.zeros(total.shape, jnp.float32)
    slots = sources[0].shape[0]
    for s, source in enumerate(sources):
        live = info[s, 2 * slots if side == 0 else 3 * slots]
        for slot in range(slots):
            if side == 0:
                y, x, t = own_spot(info, s, slot)
                mine, spot = y == here[2], lax.rem(x - here[3] + 4, 4) * 4 + t
            else:
                z, core, u = (info[s, n * slots + slot] for n in range(3))
                mine, spot = core == here[1], lax.rem(z - here[0] + 4, 4) * 4 + u

            @pl.when((slot < live) & mine)
            def _():
                total[spot] += source[slot].astype(jnp.float32)

    own[...] = total[pl.ds(0, 4)]
    for n, far in enumerate((far1, far2, far3)):
        far[...] = total[pl.ds(4 * n + 4, 4)].astype(jnp.bfloat16)


def fold_slots(side, info, here, sources):
    _, tile, width = sources[0].shape
    smem = pl.BlockSpec(memory_space=pltpu.SMEM)
    vmem = pl.BlockSpec(memory_space=pltpu.VMEM)
    far = jax.ShapeDtypeStruct((4, tile, width), jnp.bfloat16)
    return pl.pallas_call(
        functools.partial(fold_kernel, side),
        out_shape=[jax.ShapeDtypeStruct((4, tile, width), jnp.float32)] + [far] * 3,
        in_specs=[smem] * 2 + [vmem] * len(sources),
        out_specs=[vmem] * 4,
        scratch_shapes=[pltpu.VMEM((16, tile, width), jnp.float32)],
        compiler_params=pltpu.CompilerParams(vmem_limit_bytes=16 * 1024 * 1024),
    )(info, here, *sources)


def shift(value, axis, step):
    size = lax.axis_size(axis)
    return lax.ppermute(value, axis, [(i, (i + step) % size) for i in range(size)])


def ring(value, axis):
    return [shift(value, axis, s) for s in range(1, lax.axis_size(axis))]


def after(value, *others):
    return lax.optimization_barrier((value,) + others)[0]


def low_parts(value, count):
    parts = []
    for _ in range(count):
        parts.append(value.astype(jnp.bfloat16))
        value = value - parts[-1].astype(jnp.float32)
    return parts


def per_device(
    single, left_weight, right_weight, bin_weight, bin_bias, block_tiles, block_count, teacher
):
    slots, bins, tile = teacher.shape[1:4]
    devices = lax.axis_size(AXES)
    own_tiles = block_tiles[0]
    left_wide = left_weight.astype(jnp.float32)
    right_wide = right_weight.astype(jnp.float32)
    info = jnp.concatenate([own_tiles.reshape(1, -1), block_count[None]], axis=1)
    left_local = jnp.dot(single, left_weight, preferred_element_type=jnp.float32).astype(
        jnp.bfloat16
    )
    rows_dev, width = left_local.shape
    left_local = left_local.reshape(-1, tile, width)
    here = jnp.stack([lax.axis_index(a) for a in AXES]).astype(jnp.int32)
    z, core, y = here[0], here[1], here[2]
    left_near = [left_local] + ring(left_local, "x")
    right_local = jnp.dot(after(single, left_near[1]), right_weight, preferred_element_type=jnp.float32).astype(
        jnp.bfloat16
    )
    right_local = right_local.reshape(-1, tile, width)
    right_ring = ring(right_local, "z")
    info_first = after(info, left_local)
    info_y = jnp.concatenate([info_first] + ring(info_first, "y"))
    picked = pick_tiles(info_y, here, left_near)
    left_from = [picked[0]] + [shift(picked[s], "y", s) for s in (1, 2, 3)]
    row, col = own_tiles[:, 0], own_tiles[:, 1]
    right_ring = after(right_ring, *left_from)
    lists = jnp.concatenate([col // 128 % 4, col // 64 % 2, col % TILES_DEV, block_count])[None]
    packed = jnp.pad(lists.astype(jnp.bfloat16), ((0, 15), (0, width - lists.shape[1])))
    right_near = jnp.concatenate(
        [part.reshape(rows_dev, width) for part in [right_local] + right_ring] + [packed]
    )
    sibling = shift(right_near, "core", 1)
    far_lists = sibling[-16:-15, : lists.shape[1]].astype(jnp.int32)
    info_core = jnp.concatenate([lists, far_lists])
    right_from = [right_near, sibling]
    place = jnp.stack(
        [
            (y - row // 16 % 4) % 4,
            (core - col // 64 % 2) % 2,
            (z - col // 128 % 4) % 4 * TILES_DEV + col % TILES_DEV,
        ],
        axis=1,
    )
    place = after(place, info_core)
    left_slots, right_slots, bins_part, cross_part = run_blocks(
        place, block_count, bin_weight, bin_bias, left_from, right_from, teacher[0]
    )
    left_ring = ring(left_slots, "y")
    right_ring = ring(right_slots, "core")
    right_rows_grad, *right_far = fold_slots(1, info_core, here, [right_slots] + right_ring)
    right_far = [shift(right_far[s - 1], "z", s) for s in (1, 2, 3)]
    left_ring = after(left_ring, *right_far)
    left_rows_grad, *left_far = fold_slots(0, info_y, here, [left_slots] + left_ring)
    for s in (1, 2, 3):
        left_rows_grad = left_rows_grad + shift(left_far[s - 1], "x", s).astype(jnp.float32)
        right_rows_grad = right_rows_grad + right_far[s - 1].astype(jnp.float32)
    left_rows_grad = left_rows_grad.reshape(rows_dev, width)
    right_rows_grad = right_rows_grad.reshape(rows_dev, width)
    single_wide = single.astype(jnp.float32)
    part_left = jnp.dot(single_wide.T, left_rows_grad, precision=lax.Precision.HIGHEST)
    part_right = jnp.dot(single_wide.T, right_rows_grad, precision=lax.Precision.HIGHEST)
    depth = part_left.shape[0]
    rows_sum = 2 * depth + bins
    chunk = 8
    last = rows_sum // chunk, rows_sum % chunk
    bf16, f32 = jnp.bfloat16, jnp.float32
    scalars = jnp.stack(low_parts(jnp.sum(cross_part), 3) + [block_count[0].astype(bf16)])
    packed = jnp.concatenate(
        [
            part_left.astype(bf16),
            part_right.astype(bf16),
            jnp.sum(bins_part, axis=1).astype(bf16),
            jnp.pad(scalars[None], ((0, chunk * devices - rows_sum - 1), (0, width - 4))),
        ]
    ).reshape(devices, chunk, width)
    mine = jnp.sum(lax.all_to_all(packed, AXES, 0, 0).astype(f32), axis=0)
    high, low = low_parts(mine, 2)
    here_last = (lax.axis_index(AXES) == last[0]) & (jnp.arange(chunk) == last[1] + 1)
    mine = jnp.where(here_last[:, None], jnp.roll(low, 1, axis=0), high)
    totals = lax.all_to_all(
        jnp.broadcast_to(mine[None], (devices, chunk, width)), AXES, 0, 0
    ).reshape(-1, width)
    scalars = jnp.sum(totals[rows_sum : rows_sum + 2].astype(f32), axis=0)
    grad_single = (
        jnp.dot(left_rows_grad, left_wide.T, precision=lax.Precision.HIGHEST)
        + jnp.dot(right_rows_grad, right_wide.T, precision=lax.Precision.HIGHEST)
    ).astype(jnp.bfloat16)
    grad_left = totals[:depth].astype(f32) / devices
    grad_right = totals[depth : 2 * depth].astype(f32) / devices
    grad_bin = totals[2 * depth : rows_sum].T.astype(f32) / devices
    cross_total = scalars[0] + scalars[1] + scalars[2]
    loss_value = cross_total / (scalars[3] * (tile * tile))
    return (grad_single, grad_left, grad_right, grad_bin, loss_value)


def solution(mesh):
    torus = Mesh(mesh.devices.reshape(4, 2, 4, 4), AXES)
    return jax.shard_map(
        per_device,
        mesh=torus,
        in_specs=(
            P(AXES, None),
            P(),
            P(),
            P(),
            P(),
            P(AXES, None, None),
            P(AXES),
            P(AXES, None, None, None, None),
        ),
        out_specs=(P(AXES, None), P(), P(), P(), P()),
        check_vma=False,
    )
```

```python
import functools
import jax
import jax.numpy as jnp
from jax import lax
from jax.experimental import pallas as pl
from jax.experimental.pallas import tpu as pltpu
from jax.sharding import Mesh
from jax.sharding import PartitionSpec as P

GROUP_SCORES = 64
GROUP_SOFT = 16
GROUP_GRADS = 64


def blocks_kernel(
    place, count, bias, w_turned, w_plain, left0, left1, left2, left3, right0, right1, teacher,
    left_grads, right_grads, bin_out, cross_out,
    w_rows, w_wide, w_cols, left_tiles, right_tiles, target, logit, left_turn, right_turn, left_sum, right_sum,
    tile_sem, target_sem,
):
    left_from = (left0, left1, left2, left3)
    right_from = (right0, right1)
    slots, bins, tile, width = teacher.shape
    live = count[0]

    def target_copy(slot):
        return pltpu.make_async_copy(
            teacher.at[slot], target.at[lax.rem(slot, 2)], target_sem.at[lax.rem(slot, 2)]
        )

    def left_copy(slot, n):
        return pltpu.make_async_copy(
            left_from[n].at[slot], left_tiles.at[slot], tile_sem.at[slot, 0]
        )

    def right_copy(slot, n):
        return pltpu.make_async_copy(
            right_from[n].at[pl.ds(pl.multiple_of(place[slot, 2] * tile, tile), tile)],
            right_tiles.at[slot], tile_sem.at[slot, 1]
        )

    for slot in range(slots):
        for n in range(len(left_from)):

            @pl.when((slot < live) & (place[slot, 0] == n))
            def _():
                left_copy(slot, n).start()

        for n in range(len(right_from)):

            @pl.when((slot < live) & (place[slot, 1] == n))
            def _():
                right_copy(slot, n).start()

    target_copy(0).start()
    for k in range(bins):
        row = w_turned[k : k + 1, :]
        w_wide[k] = jnp.broadcast_to(row, (8, width))
        w_rows[k] = jnp.broadcast_to(row, (16, width)).astype(jnp.bfloat16)
        w_cols[k] = jnp.broadcast_to(w_plain[:, k : k + 1], (width, tile)).astype(jnp.bfloat16)
    bin_out[...] = jnp.zeros(bin_out.shape, jnp.float32)
    cross_out[...] = jnp.zeros(cross_out.shape, jnp.float32)

    def block(slot, _):
        buf = lax.rem(slot, 2)

        @pl.when(slot + 1 < live)
        def _():
            target_copy(slot + 1).start()

        left_copy(slot, 0).wait()
        right_copy(slot, 0).wait()
        left = left_tiles[slot]
        right = right_tiles[slot]
        left_turn[...] = left.T
        right_turn[...] = right.T
        left_sum[...] = jnp.zeros(left_sum.shape, jnp.float32)
        right_sum[...] = jnp.zeros(right_sum.shape, jnp.float32)

        def scores(g, highest):
            left = left_tiles[slot].reshape(tile // 16, 16, width)
            for j in range(GROUP_SCORES):
                k = g * GROUP_SCORES + j
                scaled = (left * w_rows[k][None]).reshape(tile, width)
                value = jnp.dot(scaled, right_turn[...], preferred_element_type=jnp.float32)
                value = value + bias[k]
                logit[k] = value
                highest = jnp.maximum(highest, value)
            return highest

        highest = lax.fori_loop(
            0, bins // GROUP_SCORES, scores, jnp.full((tile, tile), -jnp.inf, jnp.float32)
        )
        target_copy(slot).wait()

        STEP = 32
        ratios = []
        for p in range(0, tile, STEP):
            rows = pl.ds(p, STEP)
            top = highest[p : p + STEP]

            def soft(g, carried):
                total, mass, cross = carried
                for j in range(GROUP_SOFT):
                    k = g * GROUP_SOFT + j
                    value = logit[k, rows, :] - top
                    power = jnp.exp(value)
                    goal = target[buf, k, rows, :].astype(jnp.float32)
                    total = total + power
                    mass = mass + goal
                    cross = cross + goal * value
                    logit[k, rows, :] = power
                return total, mass, cross

            zero = jnp.zeros((STEP, tile), jnp.float32)
            total, mass, cross = lax.fori_loop(0, bins // GROUP_SOFT, soft, (zero, zero, zero))
            cross = mass * jnp.log(total) - cross
            cross_out[...] += cross.reshape(STEP // 8, 8, tile).sum(0)
            ratios.append(mass / total)
        ratio = jnp.concatenate(ratios, 0)

        def grads(g, _):
            left_wide = left_tiles[slot].astype(jnp.float32)
            pieces, scales = [], []
            left_part = jnp.zeros((tile, width), jnp.float32)
            for j in range(GROUP_GRADS):
                k = g * GROUP_GRADS + j
                grad = logit[k] * ratio - target[buf, k].astype(jnp.float32)
                grad = grad.astype(jnp.bfloat16)
                mixed = jnp.dot(grad, right_tiles[slot], preferred_element_type=jnp.float32)
                left_part = left_part + (
                    mixed.reshape(tile // 8, 8, width) * w_wide[k][None]
                ).reshape(tile, width)
                bin_out[k] += (mixed * left_wide).reshape(tile // 8, 8, width).sum(0)
                pieces.append(grad)
                scales.append(left_turn[...] * w_cols[k])
            left_sum[...] += left_part
            right_sum[...] += jnp.dot(
                jnp.concatenate(scales, 1),
                jnp.concatenate(pieces, 0),
                preferred_element_type=jnp.float32,
            )
            return 0

        lax.fori_loop(0, bins // GROUP_GRADS, grads, 0)
        left_grads[slot] = left_sum[...].astype(jnp.bfloat16)
        right_grads[slot] = right_sum[...].T.astype(jnp.bfloat16)
        return 0

    lax.fori_loop(0, live, block, 0)


def run_blocks(place, count, bin_weight, bin_bias, left_from, right_from, teacher):
    slots, bins, tile, _ = teacher.shape
    width = bin_weight.shape[0]
    wide = bin_weight.astype(jnp.float32)
    smem = pl.BlockSpec(memory_space=pltpu.SMEM)
    vmem = pl.BlockSpec(memory_space=pltpu.VMEM)
    hbm = pl.BlockSpec(memory_space=pl.ANY)
    f32, bf16 = jnp.float32, jnp.bfloat16
    piece = jax.ShapeDtypeStruct((slots, tile, width), bf16)
    return pl.pallas_call(
        blocks_kernel,
        out_shape=[piece] * 2
        + [
            jax.ShapeDtypeStruct((bins, 8, width), f32),
            jax.ShapeDtypeStruct((8, tile), f32),
        ],
        in_specs=[smem] * 3 + [vmem] * 2 + [hbm] * 7,
        out_specs=[vmem] * 4,
        scratch_shapes=[
            pltpu.VMEM((bins, 16, width), bf16),
            pltpu.VMEM((bins, 8, width), f32),
            pltpu.VMEM((bins, width, tile), bf16),
            pltpu.VMEM((slots, tile, width), bf16),
            pltpu.VMEM((slots, tile, width), bf16),
            pltpu.VMEM((2, bins, tile, tile), bf16),
            pltpu.VMEM((bins, tile, tile), f32),
            pltpu.VMEM((width, tile), bf16),
            pltpu.VMEM((width, tile), bf16),
            pltpu.VMEM((tile, width), f32),
            pltpu.VMEM((width, tile), f32),
            pltpu.SemaphoreType.DMA((slots, 2)),
            pltpu.SemaphoreType.DMA((2,)),
        ],
        compiler_params=pltpu.CompilerParams(vmem_limit_bytes=48 * 1024 * 1024),
        cost_estimate=pl.CostEstimate(
            flops=6 * 8 * 64 * 128**3, bytes_accessed=20 * 2**20, transcendentals=8 * 2**20
        ),
    )(place, count, bin_bias, wide.T, wide, *left_from, *right_from, teacher)


AXES = ("z", "core", "y", "x")
TILES_DEV = 4


def own_spot(info, s, slot):
    row = info[s, 2 * slot]
    return lax.rem(row // 16, 4), lax.rem(row // 4, 4), lax.rem(row, 4)


def pick_kernel(info, here, near0, near1, near2, near3, out0, out1, out2, out3, bank):
    outs = (out0, out1, out2, out3)
    for n, near in enumerate((near0, near1, near2, near3)):
        bank[pl.ds(4 * n, 4)] = near[...]
    slots = out0.shape[0]
    for s in range(4):
        for slot in range(slots):
            _, x, t = own_spot(info, s, slot)
            spot = lax.rem(here[3] - x + 4, 4) * 4 + t
            outs[(4 - s) % 4][slot] = bank[spot]


def pick_tiles(info, here, near):
    slots = (info.shape[1] - 1) // 2
    _, tile, width = near[0].shape
    smem = pl.BlockSpec(memory_space=pltpu.SMEM)
    vmem = pl.BlockSpec(memory_space=pltpu.VMEM)
    return pl.pallas_call(
        pick_kernel,
        out_shape=[jax.ShapeDtypeStruct((slots, tile, width), near[0].dtype)] * 4,
        in_specs=[smem] * 2 + [vmem] * 4,
        out_specs=[vmem] * 4,
        scratch_shapes=[pltpu.VMEM((16, tile, width), near[0].dtype)],
        compiler_params=pltpu.CompilerParams(vmem_limit_bytes=16 * 1024 * 1024),
    )(info, here, *near)


def fold_kernel(side, info, here, *refs):
    sources, (own, far1, far2, far3, total) = refs[:-5], refs[-5:]
    total[...] = jnp.zeros(total.shape, jnp.float32)
    slots = sources[0].shape[0]
    for s, source in enumerate(sources):
        live = info[s, 2 * slots if side == 0 else 3 * slots]
        for slot in range(slots):
            if side == 0:
                y, x, t = own_spot(info, s, slot)
                mine, spot = y == here[2], lax.rem(x - here[3] + 4, 4) * 4 + t
            else:
                z, core, u = (info[s, n * slots + slot] for n in range(3))
                mine, spot = core == here[1], lax.rem(z - here[0] + 4, 4) * 4 + u

            @pl.when((slot < live) & mine)
            def _():
                total[spot] += source[slot].astype(jnp.float32)

    own[...] = total[pl.ds(0, 4)]
    for n, far in enumerate((far1, far2, far3)):
        far[...] = total[pl.ds(4 * n + 4, 4)].astype(jnp.bfloat16)


def fold_slots(side, info, here, sources):
    _, tile, width = sources[0].shape
    smem = pl.BlockSpec(memory_space=pltpu.SMEM)
    vmem = pl.BlockSpec(memory_space=pltpu.VMEM)
    far = jax.ShapeDtypeStruct((4, tile, width), jnp.bfloat16)
    return pl.pallas_call(
        functools.partial(fold_kernel, side),
        out_shape=[jax.ShapeDtypeStruct((4, tile, width), jnp.float32)] + [far] * 3,
        in_specs=[smem] * 2 + [vmem] * len(sources),
        out_specs=[vmem] * 4,
        scratch_shapes=[pltpu.VMEM((16, tile, width), jnp.float32)],
        compiler_params=pltpu.CompilerParams(vmem_limit_bytes=16 * 1024 * 1024),
    )(info, here, *sources)


def shift(value, axis, step):
    size = lax.axis_size(axis)
    return lax.ppermute(value, axis, [(i, (i + step) % size) for i in range(size)])


def ring(value, axis):
    return [shift(value, axis, s) for s in range(1, lax.axis_size(axis))]


def after(value, *others):
    return lax.optimization_barrier((value,) + others)[0]


def low_parts(value, count):
    parts = []
    for _ in range(count):
        parts.append(value.astype(jnp.bfloat16))
        value = value - parts[-1].astype(jnp.float32)
    return parts


def per_device(
    single, left_weight, right_weight, bin_weight, bin_bias, block_tiles, block_count, teacher
):
    slots, bins, tile = teacher.shape[1:4]
    devices = lax.axis_size(AXES)
    own_tiles = block_tiles[0]
    left_wide = left_weight.astype(jnp.float32)
    right_wide = right_weight.astype(jnp.float32)
    info = jnp.concatenate([own_tiles.reshape(1, -1), block_count[None]], axis=1)
    left_local = jnp.dot(single, left_weight, preferred_element_type=jnp.float32).astype(
        jnp.bfloat16
    )
    rows_dev, width = left_local.shape
    left_local = left_local.reshape(-1, tile, width)
    here = jnp.stack([lax.axis_index(a) for a in AXES]).astype(jnp.int32)
    z, core, y = here[0], here[1], here[2]
    left_near = [left_local] + ring(left_local, "x")
    right_local = jnp.dot(after(single, left_near[1]), right_weight, preferred_element_type=jnp.float32).astype(
        jnp.bfloat16
    )
    right_local = right_local.reshape(-1, tile, width)
    right_ring = ring(right_local, "z")
    info_first = after(info, left_local)
    info_y = jnp.concatenate([info_first] + ring(info_first, "y"))
    picked = pick_tiles(info_y, here, left_near)
    left_from = [picked[0]] + [shift(picked[s], "y", s) for s in (1, 2, 3)]
    row, col = own_tiles[:, 0], own_tiles[:, 1]
    right_ring = after(right_ring, *left_from)
    lists = jnp.concatenate([col // 128 % 4, col // 64 % 2, col % TILES_DEV, block_count])[None]
    packed = jnp.pad(lists.astype(jnp.bfloat16), ((0, 15), (0, width - lists.shape[1])))
    right_near = jnp.concatenate(
        [part.reshape(rows_dev, width) for part in [right_local] + right_ring] + [packed]
    )
    sibling = shift(right_near, "core", 1)
    far_lists = sibling[-16:-15, : lists.shape[1]].astype(jnp.int32)
    info_core = jnp.concatenate([lists, far_lists])
    right_from = [right_near, sibling]
    place = jnp.stack(
        [
            (y - row // 16 % 4) % 4,
            (core - col // 64 % 2) % 2,
            (z - col // 128 % 4) % 4 * TILES_DEV + col % TILES_DEV,
        ],
        axis=1,
    )
    place = after(place, info_core)
    left_slots, right_slots, bins_part, cross_part = run_blocks(
        place, block_count, bin_weight, bin_bias, left_from, right_from, teacher[0]
    )
    left_ring = ring(left_slots, "y")
    right_ring = ring(right_slots, "core")
    right_rows_grad, *right_far = fold_slots(1, info_core, here, [right_slots] + right_ring)
    right_far = [shift(right_far[s - 1], "z", s) for s in (1, 2, 3)]
    left_ring = after(left_ring, *right_far)
    left_rows_grad, *left_far = fold_slots(0, info_y, here, [left_slots] + left_ring)
    for s in (1, 2, 3):
        left_rows_grad = left_rows_grad + shift(left_far[s - 1], "x", s).astype(jnp.float32)
        right_rows_grad = right_rows_grad + right_far[s - 1].astype(jnp.float32)
    left_rows_grad = left_rows_grad.reshape(rows_dev, width)
    right_rows_grad = right_rows_grad.reshape(rows_dev, width)
    single_wide = single.astype(jnp.float32)
    part_left = jnp.dot(single_wide.T, left_rows_grad, precision=lax.Precision.HIGHEST)
    part_right = jnp.dot(single_wide.T, right_rows_grad, precision=lax.Precision.HIGHEST)
    depth = part_left.shape[0]
    rows_sum = 2 * depth + bins
    chunk = rows_sum // devices + 1
    last = rows_sum // chunk, rows_sum % chunk
    bf16, f32 = jnp.bfloat16, jnp.float32
    scalars = jnp.stack(low_parts(jnp.sum(cross_part), 3) + [block_count[0].astype(bf16)])
    packed = jnp.concatenate(
        [
            part_left.astype(bf16),
            part_right.astype(bf16),
            jnp.sum(bins_part, axis=1).astype(bf16),
            jnp.pad(scalars[None], ((0, chunk * devices - rows_sum - 1), (0, width - 4))),
        ]
    ).reshape(devices, chunk, width)
    mine = jnp.sum(lax.all_to_all(packed, AXES, 0, 0).astype(f32), axis=0)
    high, low = low_parts(mine, 2)
    mine = jnp.concatenate([high, low[last[1] : last[1] + 1]])
    totals = lax.all_to_all(
        jnp.broadcast_to(mine[None], (devices, chunk + 1, width)), AXES, 0, 0
    ).astype(f32)
    scalars = totals[last[0], last[1]] + totals[last[0], chunk]
    totals = totals[:, :chunk].reshape(-1, width)
    grad_single = (
        jnp.dot(left_rows_grad, left_wide.T, precision=lax.Precision.HIGHEST)
        + jnp.dot(right_rows_grad, right_wide.T, precision=lax.Precision.HIGHEST)
    ).astype(jnp.bfloat16)
    grad_left = totals[:depth] / devices
    grad_right = totals[depth : 2 * depth] / devices
    grad_bin = totals[2 * depth : rows_sum].T / devices
    cross_total = scalars[0] + scalars[1] + scalars[2]
    loss_value = cross_total / (scalars[3] * (tile * tile))
    return (grad_single, grad_left, grad_right, grad_bin, loss_value)


def solution(mesh):
    torus = Mesh(mesh.devices.reshape(4, 2, 4, 4), AXES)
    return jax.shard_map(
        per_device,
        mesh=torus,
        in_specs=(
            P(AXES, None),
            P(),
            P(),
            P(),
            P(),
            P(AXES, None, None),
            P(AXES),
            P(AXES, None, None, None, None),
        ),
        out_specs=(P(AXES, None), P(), P(), P(), P()),
        check_vma=False,
    )
```

```python
import functools
import jax
import jax.numpy as jnp
from jax import lax
from jax.experimental import pallas as pl
from jax.experimental.pallas import tpu as pltpu
from jax.sharding import Mesh
from jax.sharding import PartitionSpec as P

GROUP_SCORES = 64
GROUP_SOFT = 64
GROUP_GRADS = 64


def blocks_kernel(
    place, count, bias, w_turned, w_plain, left0, left1, left2, left3, right0, right1, teacher,
    left_grads, right_grads, bin_out, cross_out,
    w_rows, w_wide, w_cols, left_tiles, right_tiles, target, logit, left_turn, right_turn, left_sum, right_sum,
    tile_sem, target_sem,
):
    left_from = (left0, left1, left2, left3)
    right_from = (right0, right1)
    slots, bins, tile, width = teacher.shape
    live = count[0]

    def target_copy(slot):
        return pltpu.make_async_copy(
            teacher.at[slot], target.at[lax.rem(slot, 2)], target_sem.at[lax.rem(slot, 2)]
        )

    def left_copy(slot, n):
        return pltpu.make_async_copy(
            left_from[n].at[slot], left_tiles.at[slot], tile_sem.at[slot, 0]
        )

    def right_copy(slot, n):
        return pltpu.make_async_copy(
            right_from[n].at[pl.ds(pl.multiple_of(place[slot, 2] * tile, tile), tile)],
            right_tiles.at[slot], tile_sem.at[slot, 1]
        )

    for slot in range(slots):
        for n in range(len(left_from)):

            @pl.when((slot < live) & (place[slot, 0] == n))
            def _():
                left_copy(slot, n).start()

        for n in range(len(right_from)):

            @pl.when((slot < live) & (place[slot, 1] == n))
            def _():
                right_copy(slot, n).start()

    target_copy(0).start()
    for k in range(bins):
        row = w_turned[k : k + 1, :]
        w_wide[k] = jnp.broadcast_to(row, (8, width))
        w_rows[k] = jnp.broadcast_to(row, (16, width)).astype(jnp.bfloat16)
        w_cols[k] = jnp.broadcast_to(w_plain[:, k : k + 1], (width, tile)).astype(jnp.bfloat16)
    bin_out[...] = jnp.zeros(bin_out.shape, jnp.float32)
    cross_out[...] = jnp.zeros(cross_out.shape, jnp.float32)

    def block(slot, _):
        buf = lax.rem(slot, 2)

        @pl.when(slot + 1 < live)
        def _():
            target_copy(slot + 1).start()

        left_copy(slot, 0).wait()
        right_copy(slot, 0).wait()
        left = left_tiles[slot]
        right = right_tiles[slot]
        left_turn[...] = left.T
        right_turn[...] = right.T
        left_sum[...] = jnp.zeros(left_sum.shape, jnp.float32)
        right_sum[...] = jnp.zeros(right_sum.shape, jnp.float32)

        def scores(g, highest):
            left = left_tiles[slot].reshape(tile // 16, 16, width)
            for j in range(GROUP_SCORES):
                k = g * GROUP_SCORES + j
                scaled = (left * w_rows[k][None]).reshape(tile, width)
                value = jnp.dot(scaled, right_turn[...], preferred_element_type=jnp.float32)
                value = value + bias[k]
                logit[k] = value
                highest = jnp.maximum(highest, value)
            return highest

        highest = lax.fori_loop(
            0, bins // GROUP_SCORES, scores, jnp.full((tile, tile), -jnp.inf, jnp.float32)
        )
        target_copy(slot).wait()

        STEP = 32
        ratios = []
        for p in range(0, tile, STEP):
            rows = pl.ds(p, STEP)
            top = highest[p : p + STEP]

            def soft(g, carried):
                total, mass, cross = carried
                for j in range(GROUP_SOFT):
                    k = g * GROUP_SOFT + j
                    value = logit[k, rows, :] - top
                    power = jnp.exp(value)
                    goal = target[buf, k, rows, :].astype(jnp.float32)
                    total = total + power
                    mass = mass + goal
                    cross = cross + goal * value
                    logit[k, rows, :] = power
                return total, mass, cross

            zero = jnp.zeros((STEP, tile), jnp.float32)
            total, mass, cross = lax.fori_loop(0, bins // GROUP_SOFT, soft, (zero, zero, zero))
            cross = mass * jnp.log(total) - cross
            cross_out[...] += cross.reshape(STEP // 8, 8, tile).sum(0)
            ratios.append(mass / total)
        ratio = jnp.concatenate(ratios, 0)

        def grads(g, _):
            left_wide = left_tiles[slot].astype(jnp.float32)
            pieces, scales = [], []
            left_part = jnp.zeros((tile, width), jnp.float32)
            for j in range(GROUP_GRADS):
                k = g * GROUP_GRADS + j
                grad = logit[k] * ratio - target[buf, k].astype(jnp.float32)
                grad = grad.astype(jnp.bfloat16)
                mixed = jnp.dot(grad, right_tiles[slot], preferred_element_type=jnp.float32)
                left_part = left_part + (
                    mixed.reshape(tile // 8, 8, width) * w_wide[k][None]
                ).reshape(tile, width)
                bin_out[k] += (mixed * left_wide).reshape(tile // 8, 8, width).sum(0)
                pieces.append(grad)
                scales.append(left_turn[...] * w_cols[k])
            left_sum[...] += left_part
            right_sum[...] += jnp.dot(
                jnp.concatenate(scales, 1),
                jnp.concatenate(pieces, 0),
                preferred_element_type=jnp.float32,
            )
            return 0

        lax.fori_loop(0, bins // GROUP_GRADS, grads, 0)
        left_grads[slot] = left_sum[...].astype(jnp.bfloat16)
        right_grads[slot] = right_sum[...].T.astype(jnp.bfloat16)
        return 0

    lax.fori_loop(0, live, block, 0)


def run_blocks(place, count, bin_weight, bin_bias, left_from, right_from, teacher):
    slots, bins, tile, _ = teacher.shape
    width = bin_weight.shape[0]
    wide = bin_weight.astype(jnp.float32)
    smem = pl.BlockSpec(memory_space=pltpu.SMEM)
    vmem = pl.BlockSpec(memory_space=pltpu.VMEM)
    hbm = pl.BlockSpec(memory_space=pl.ANY)
    f32, bf16 = jnp.float32, jnp.bfloat16
    piece = jax.ShapeDtypeStruct((slots, tile, width), bf16)
    return pl.pallas_call(
        blocks_kernel,
        out_shape=[piece] * 2
        + [
            jax.ShapeDtypeStruct((bins, 8, width), f32),
            jax.ShapeDtypeStruct((8, tile), f32),
        ],
        in_specs=[smem] * 3 + [vmem] * 2 + [hbm] * 7,
        out_specs=[vmem] * 4,
        scratch_shapes=[
            pltpu.VMEM((bins, 16, width), bf16),
            pltpu.VMEM((bins, 8, width), f32),
            pltpu.VMEM((bins, width, tile), bf16),
            pltpu.VMEM((slots, tile, width), bf16),
            pltpu.VMEM((slots, tile, width), bf16),
            pltpu.VMEM((2, bins, tile, tile), bf16),
            pltpu.VMEM((bins, tile, tile), f32),
            pltpu.VMEM((width, tile), bf16),
            pltpu.VMEM((width, tile), bf16),
            pltpu.VMEM((tile, width), f32),
            pltpu.VMEM((width, tile), f32),
            pltpu.SemaphoreType.DMA((slots, 2)),
            pltpu.SemaphoreType.DMA((2,)),
        ],
        compiler_params=pltpu.CompilerParams(vmem_limit_bytes=48 * 1024 * 1024),
        cost_estimate=pl.CostEstimate(
            flops=6 * 8 * 64 * 128**3, bytes_accessed=20 * 2**20, transcendentals=8 * 2**20
        ),
    )(place, count, bin_bias, wide.T, wide, *left_from, *right_from, teacher)


AXES = ("z", "core", "y", "x")
TILES_DEV = 4


def own_spot(info, s, slot):
    row = info[s, 2 * slot]
    return lax.rem(row // 16, 4), lax.rem(row // 4, 4), lax.rem(row, 4)


def pick_kernel(info, here, near0, near1, near2, near3, out0, out1, out2, out3, bank):
    outs = (out0, out1, out2, out3)
    for n, near in enumerate((near0, near1, near2, near3)):
        bank[pl.ds(4 * n, 4)] = near[...]
    slots = out0.shape[0]
    for s in range(4):
        for slot in range(slots):
            _, x, t = own_spot(info, s, slot)
            spot = lax.rem(here[3] - x + 4, 4) * 4 + t
            outs[(4 - s) % 4][slot] = bank[spot]


def pick_tiles(info, here, near):
    slots = (info.shape[1] - 1) // 2
    _, tile, width = near[0].shape
    smem = pl.BlockSpec(memory_space=pltpu.SMEM)
    vmem = pl.BlockSpec(memory_space=pltpu.VMEM)
    return pl.pallas_call(
        pick_kernel,
        out_shape=[jax.ShapeDtypeStruct((slots, tile, width), near[0].dtype)] * 4,
        in_specs=[smem] * 2 + [vmem] * 4,
        out_specs=[vmem] * 4,
        scratch_shapes=[pltpu.VMEM((16, tile, width), near[0].dtype)],
        compiler_params=pltpu.CompilerParams(vmem_limit_bytes=16 * 1024 * 1024),
    )(info, here, *near)


def fold_kernel(side, info, here, *refs):
    sources, (own, far1, far2, far3, total) = refs[:-5], refs[-5:]
    total[...] = jnp.zeros(total.shape, jnp.float32)
    slots = sources[0].shape[0]
    for s, source in enumerate(sources):
        live = info[s, 2 * slots if side == 0 else 3 * slots]
        for slot in range(slots):
            if side == 0:
                y, x, t = own_spot(info, s, slot)
                mine, spot = y == here[2], lax.rem(x - here[3] + 4, 4) * 4 + t
            else:
                z, core, u = (info[s, n * slots + slot] for n in range(3))
                mine, spot = core == here[1], lax.rem(z - here[0] + 4, 4) * 4 + u

            @pl.when((slot < live) & mine)
            def _():
                total[spot] += source[slot].astype(jnp.float32)

    own[...] = total[pl.ds(0, 4)]
    for n, far in enumerate((far1, far2, far3)):
        far[...] = total[pl.ds(4 * n + 4, 4)].astype(jnp.bfloat16)


def fold_slots(side, info, here, sources):
    _, tile, width = sources[0].shape
    smem = pl.BlockSpec(memory_space=pltpu.SMEM)
    vmem = pl.BlockSpec(memory_space=pltpu.VMEM)
    far = jax.ShapeDtypeStruct((4, tile, width), jnp.bfloat16)
    return pl.pallas_call(
        functools.partial(fold_kernel, side),
        out_shape=[jax.ShapeDtypeStruct((4, tile, width), jnp.float32)] + [far] * 3,
        in_specs=[smem] * 2 + [vmem] * len(sources),
        out_specs=[vmem] * 4,
        scratch_shapes=[pltpu.VMEM((16, tile, width), jnp.float32)],
        compiler_params=pltpu.CompilerParams(vmem_limit_bytes=16 * 1024 * 1024),
    )(info, here, *sources)


def shift(value, axis, step):
    size = lax.axis_size(axis)
    return lax.ppermute(value, axis, [(i, (i + step) % size) for i in range(size)])


def ring(value, axis):
    return [shift(value, axis, s) for s in range(1, lax.axis_size(axis))]


def after(value, *others):
    return lax.optimization_barrier((value,) + others)[0]


def low_parts(value, count):
    parts = []
    for _ in range(count):
        parts.append(value.astype(jnp.bfloat16))
        value = value - parts[-1].astype(jnp.float32)
    return parts


def per_device(
    single, left_weight, right_weight, bin_weight, bin_bias, block_tiles, block_count, teacher
):
    slots, bins, tile = teacher.shape[1:4]
    devices = lax.axis_size(AXES)
    own_tiles = block_tiles[0]
    left_wide = left_weight.astype(jnp.float32)
    right_wide = right_weight.astype(jnp.float32)
    info = jnp.concatenate([own_tiles.reshape(1, -1), block_count[None]], axis=1)
    left_local = jnp.dot(single, left_weight, preferred_element_type=jnp.float32).astype(
        jnp.bfloat16
    )
    rows_dev, width = left_local.shape
    left_local = left_local.reshape(-1, tile, width)
    here = jnp.stack([lax.axis_index(a) for a in AXES]).astype(jnp.int32)
    z, core, y = here[0], here[1], here[2]
    left_near = [left_local] + ring(left_local, "x")
    right_local = jnp.dot(after(single, left_near[1]), right_weight, preferred_element_type=jnp.float32).astype(
        jnp.bfloat16
    )
    right_local = right_local.reshape(-1, tile, width)
    right_ring = ring(right_local, "z")
    info_first = after(info, left_local)
    info_y = jnp.concatenate([info_first] + ring(info_first, "y"))
    picked = pick_tiles(info_y, here, left_near)
    left_from = [picked[0]] + [shift(picked[s], "y", s) for s in (1, 2, 3)]
    row, col = own_tiles[:, 0], own_tiles[:, 1]
    right_ring = after(right_ring, *left_from)
    lists = jnp.concatenate([col // 128 % 4, col // 64 % 2, col % TILES_DEV, block_count])[None]
    packed = jnp.pad(lists.astype(jnp.bfloat16), ((0, 15), (0, width - lists.shape[1])))
    right_near = jnp.concatenate(
        [part.reshape(rows_dev, width) for part in [right_local] + right_ring] + [packed]
    )
    sibling = shift(right_near, "core", 1)
    far_lists = sibling[-16:-15, : lists.shape[1]].astype(jnp.int32)
    info_core = jnp.concatenate([lists, far_lists])
    right_from = [right_near, sibling]
    place = jnp.stack(
        [
            (y - row // 16 % 4) % 4,
            (core - col // 64 % 2) % 2,
            (z - col // 128 % 4) % 4 * TILES_DEV + col % TILES_DEV,
        ],
        axis=1,
    )
    place = after(place, info_core)
    left_slots, right_slots, bins_part, cross_part = run_blocks(
        place, block_count, bin_weight, bin_bias, left_from, right_from, teacher[0]
    )
    left_ring = ring(left_slots, "y")
    right_ring = ring(right_slots, "core")
    right_rows_grad, *right_far = fold_slots(1, info_core, here, [right_slots] + right_ring)
    right_far = [shift(right_far[s - 1], "z", s) for s in (1, 2, 3)]
    left_ring = after(left_ring, *right_far)
    left_rows_grad, *left_far = fold_slots(0, info_y, here, [left_slots] + left_ring)
    for s in (1, 2, 3):
        left_rows_grad = left_rows_grad + shift(left_far[s - 1], "x", s).astype(jnp.float32)
        right_rows_grad = right_rows_grad + right_far[s - 1].astype(jnp.float32)
    left_rows_grad = left_rows_grad.reshape(rows_dev, width)
    right_rows_grad = right_rows_grad.reshape(rows_dev, width)
    single_wide = single.astype(jnp.float32)
    part_left = jnp.dot(single_wide.T, left_rows_grad, precision=lax.Precision.HIGHEST)
    part_right = jnp.dot(single_wide.T, right_rows_grad, precision=lax.Precision.HIGHEST)
    depth = part_left.shape[0]
    rows_sum = 2 * depth + bins
    chunk = rows_sum // devices + 1
    last = rows_sum // chunk, rows_sum % chunk
    bf16, f32 = jnp.bfloat16, jnp.float32
    scalars = jnp.stack(low_parts(jnp.sum(cross_part), 3) + [block_count[0].astype(bf16)])
    packed = jnp.concatenate(
        [
            part_left.astype(bf16),
            part_right.astype(bf16),
            jnp.sum(bins_part, axis=1).astype(bf16),
            jnp.pad(scalars[None], ((0, chunk * devices - rows_sum - 1), (0, width - 4))),
        ]
    ).reshape(devices, chunk, width)
    mine = jnp.sum(lax.all_to_all(packed, AXES, 0, 0).astype(f32), axis=0)
    high, low = low_parts(mine, 2)
    mine = jnp.concatenate([high, low[last[1] : last[1] + 1]])
    totals = lax.all_to_all(
        jnp.broadcast_to(mine[None], (devices, chunk + 1, width)), AXES, 0, 0
    ).astype(f32)
    scalars = totals[last[0], last[1]] + totals[last[0], chunk]
    totals = totals[:, :chunk].reshape(-1, width)
    grad_single = (
        jnp.dot(left_rows_grad, left_wide.T, precision=lax.Precision.HIGHEST)
        + jnp.dot(right_rows_grad, right_wide.T, precision=lax.Precision.HIGHEST)
    ).astype(jnp.bfloat16)
    grad_left = totals[:depth] / devices
    grad_right = totals[depth : 2 * depth] / devices
    grad_bin = totals[2 * depth : rows_sum].T / devices
    cross_total = scalars[0] + scalars[1] + scalars[2]
    loss_value = cross_total / (scalars[3] * (tile * tile))
    return (grad_single, grad_left, grad_right, grad_bin, loss_value)


def solution(mesh):
    torus = Mesh(mesh.devices.reshape(4, 2, 4, 4), AXES)
    return jax.shard_map(
        per_device,
        mesh=torus,
        in_specs=(
            P(AXES, None),
            P(),
            P(),
            P(),
            P(),
            P(AXES, None, None),
            P(AXES),
            P(AXES, None, None, None, None),
        ),
        out_specs=(P(AXES, None), P(), P(), P(), P()),
        check_vma=False,
    )
```
